32 devices in a mesh: dp: 2 (over y), blocks: 16 (over z, x, core).
Axes of the slice: x: 2, y: 2, z: 4, core: 2. Of those that a mesh axis runs over, the one named last changes fastest.
Arguments:
- tokens: bfloat16 [4096, 8192], P('blocks', 'dp'), may hold values from -6 to 6
- dec_bias: float32 [8192], P('dp'), may hold values from -3 to 3
- routes: int32 [4096, 2], P('blocks'), may hold values from 0 to 15, all different within a row; in each aligned block of 256 rows (0 to 255, 256 to 511, ...) at most 64 rows name the same one
- latent_picks: int32 [4096, 2, 16], P('blocks'), may hold values from 0 to 1023
- enc_weight: bfloat16 [16, 8192, 1024], P('blocks', 'dp'), may hold values from -0.0625 to 0.0625
- dec_weight: bfloat16 [16, 1024, 8192], P('blocks', None, 'dp'), may hold values from -1 to 1
- enc_bias: float32 [16, 1024], P('blocks'), may hold values from -3 to 3
Outputs:
- reconstruction: bfloat16 [4096, 8192], P('blocks', 'dp')
The draws below stay inside these ranges and needn't reach their ends.
Inputs may be any that keep to these rules, and one draw needn't show every extreme that they name: `routes`: each row names 2 different blocks; among the rows of one index of blocks no block is named by more than 64 rows, and some block by exactly 64. `latent_picks`: indices within a block; a row may name an index more than once.
All inputs are finite; a program needn't handle non-finite values.
Results may differ from the reference program's by a relative error of at most 0.0059.
Values may be sent and summed in bfloat16 or wider, within the bound.
No kernel may reach another device: no remote copies, remote signals or barrier semaphores. Data moves between devices by JAX's collectives and lax.ppermute only.
A program may use at most 64 MiB of HBM per device.

```python
import math
import jax
import jax.numpy as jnp
import numpy as np
from jax import lax

D = 8192
LAT = 1024
K_BLK = 2
KIN = 16
R = 256
NBLK = 16
CAP = 64
TOKENS = 4096


def plant(entries, own_key, low, largest):
    longest = entries.shape.index(max(entries.shape))
    spots = []
    for shift in (0, 1):
        where = [jax.random.randint(jax.random.fold_in(own_key, axis), (), 0, length) for axis, length in enumerate(entries.shape)]
        where[longest] = (where[longest] + shift) % entries.shape[longest]
        spots.append(tuple(where))
    return entries.at[spots[0]].set(low).at[spots[1]].set(largest)


def shard_levels(key, shape, split, low, top_value):
    factor_of, own = 1.0, jax.random.fold_in(key, 6)
    for dim, shards_of in split:
        draws = jnp.exp(jax.random.uniform(jax.random.fold_in(own, dim), (shards_of,), jnp.float32, low / len(split), top_value / len(split)))
        factor_of = factor_of * jnp.repeat(draws, shape[dim] // shards_of).reshape([-1 if axis == dim else 1 for axis in range(len(shape))])
    return factor_of


def routed_block(own_key, own, number, rows, amount, top, most, skew):
    order = jax.random.permutation(own_key, amount)
    heavy_load, usual = load_shares(amount, rows * top, most, skew, True), load_shares(amount, rows * top, most, skew, False)
    places = jnp.arange(amount)

    def named(tallies, offset_by):
        used = int((tallies > 0).sum())
        fixed = max(1, used // 4)
        moved = fixed + (places - fixed + offset_by * (used - fixed)) % max(1, amount - fixed)
        return jnp.zeros((amount,), jnp.int32).at[order[jnp.where(places < fixed, places, moved)]].set(jnp.asarray(tallies, jnp.int32))

    tallies = jnp.where(number % 4 == 0, named(heavy_load, number // 4), named(usual, number - number // 4 - 1))
    mixed = jax.random.permutation(jax.random.fold_in(own, 3), amount)
    giver, receiver = mixed[0:amount // 2 * 2:2], mixed[1:amount // 2 * 2:2]
    margin = jnp.minimum(tallies[giver] - 1, most - tallies[receiver]) // 2
    margin = jnp.where((giver == order[0]) | (receiver == order[0]) | (tallies[receiver] == 0), 0, jnp.maximum(margin, 0))
    moved = jax.random.randint(jax.random.fold_in(own, 4), (amount // 2,), 0, 1 << 20) % (margin + 1)
    tallies = tallies.at[giver].add(-moved).at[receiver].add(moved)
    labels = jnp.searchsorted(jnp.cumsum(tallies), jnp.arange(rows * top), side="right").astype(jnp.int32)
    table = labels.reshape(top, rows).T
    table = table[jax.random.permutation(jax.random.fold_in(own, 1), rows)]
    offset_by = jax.random.randint(jax.random.fold_in(own, 2), (rows, 1), 0, top)
    return jnp.take_along_axis(table, (jnp.arange(top)[None, :] + offset_by) % top, axis=1)


def load_shares(amount, total, most, lean, full):
    weights = [(1 << 20) // math.isqrt(grade ** lean) + 1 for grade in range(1, amount + 1)]
    largest = most if full else min(most, max(-(-total // amount), total * weights[0] // sum(weights)))
    least = 1 if total - largest >= amount - 1 else 0
    counts, spare = [largest] + [least] * (amount - 1), total - largest - least * (amount - 1)
    while spare > 0:
        movable = [i for i in range(1, amount) if counts[i] < largest] or [i for i in range(1, amount) if counts[i] < most]
        mass, budget = sum([weights[i] for i in movable]), spare
        for i in movable:
            extra = min(most - counts[i], max(1, budget * weights[i] // mass), spare)
            counts[i] = counts[i] + extra
            spare = spare - extra
    return np.array(counts)


def normal_values(stream_key, shape, deviation, bound, shards=(), held_as=jnp.bfloat16):
    values = jax.random.normal(stream_key, shape, jnp.float32) * deviation
    if len(shards) > 0:
        values = shard_levels(stream_key, shape, shards, -0.22, 0.18) * values
    return jnp.clip(values, min=-bound, max=bound).astype(held_as)


def setup_inputs(seed: int = 0) -> dict:
    splits = jax.random.split(jax.random.key(seed), 8)
    tokens = normal_values(splits[0], (TOKENS, D), 1.0, 6.0, ((0, 16), (1, 2)))
    dec_bias = normal_values(splits[1], (D,), 0.5, 3.0, ((0, 2),), jnp.float32)
    routes_keys = jax.random.split(jax.random.fold_in(splits[2], 1), TOKENS // R)
    routes_turns = jax.random.permutation(jax.random.fold_in(splits[2], 3), TOKENS // R)
    routes = jax.vmap(lambda own, number: routed_block(jax.random.fold_in(splits[2], 2), own, number, R, NBLK, K_BLK, CAP, 2))(routes_keys, routes_turns).reshape((TOKENS, K_BLK))
    latent_picks = plant(jax.random.randint(splits[3], (TOKENS, K_BLK, KIN), 0, LAT), jax.random.fold_in(splits[3], 1), 0, LAT - 1).astype(jnp.int32)
    enc_weight = normal_values(splits[4], (NBLK, D, LAT), D ** -0.5, 0.0625, ((0, 16), (1, 2)))
    dec_weight = normal_values(splits[5], (NBLK, LAT, D), (2 * KIN) ** -0.5, 1.0, ((0, 16), (2, 2)))
    enc_bias = normal_values(splits[6], (NBLK, LAT), 0.5, 3.0, ((0, 16),), jnp.float32)
    return {"tokens": tokens, "dec_bias": dec_bias, "routes": routes, "latent_picks": latent_picks, "enc_weight": enc_weight, "dec_weight": dec_weight, "enc_bias": enc_bias}


def reference(tokens, dec_bias, routes, latent_picks, enc_weight, dec_weight, enc_bias):
    centered = (tokens.astype(jnp.float32) - dec_bias).astype(jnp.bfloat16)
    tile_rows = math.gcd(TOKENS, 64)
    tile_count = TOKENS // tile_rows
    pair_count = tile_rows * K_BLK
    earlier = jnp.tril(jnp.ones((KIN, KIN), jnp.int32), -1) > 0

    def one_tile(index):
        first = (index * tile_rows).astype(jnp.int32)
        block_rows = lax.dynamic_slice_in_dim(centered, first, tile_rows, 0)
        owners = lax.dynamic_slice_in_dim(routes, first, tile_rows, 0).reshape(pair_count)
        chosen = lax.dynamic_slice_in_dim(latent_picks, first, tile_rows, 0).reshape(pair_count, KIN)
        repeated = jnp.repeat(block_rows, K_BLK, axis=0)
        columns = enc_weight[owners[:, None], :, chosen]
        pre = jnp.einsum("pkd,pd->pk", columns.astype(jnp.float32), repeated.astype(jnp.float32))
        pre = pre + enc_bias[owners[:, None], chosen]
        repeat_mask = jnp.any((chosen[:, :, None] == chosen[:, None, :]) & earlier[None], axis=2)
        active = jnp.where(repeat_mask, 0.0, jnp.maximum(pre, 0.0)).astype(jnp.bfloat16)
        active = lax.optimization_barrier(active).astype(jnp.float32)
        dec_rows = dec_weight[owners[:, None], chosen, :]
        partial_value = jnp.einsum("pk,pkd->pd", active, dec_rows.astype(jnp.float32)).astype(jnp.bfloat16)
        partial_value = lax.optimization_barrier(partial_value).astype(jnp.float32)
        summed = partial_value.reshape(tile_rows, K_BLK, D).sum(axis=1) + dec_bias
        return summed.astype(jnp.bfloat16)

    result = lax.map(one_tile, jnp.arange(tile_count, dtype=jnp.int32))
    return result.reshape(TOKENS, D)
```

```python
import functools

import jax
import jax.numpy as jnp
from jax import lax
from jax.experimental import pallas as pl
from jax.experimental.pallas import tpu as pltpu
from jax.sharding import PartitionSpec as P

BACK_CHUNKS = (1, 1, 1, 1)
SUM_CHUNKS = 2
INNER = 4
OUTER = 4
EXTRA = 128
BLOCK = 512
VMEM = 24 * 1024 * 1024
F32 = jnp.float32
BF16 = jnp.bfloat16


def flat_on_device(tokens, dec_bias, routes, latent_picks, enc_weight, dec_weight, enc_bias):
    tok_rows, quarter = tokens.shape
    top_blocks = routes.shape[1]
    pick_count = latent_picks.shape[2]
    latents = enc_weight.shape[2]
    blk_count = lax.axis_size("blocks")
    capacity = max(2, 2 * tok_rows * top_blocks // blk_count)
    slot_count = blk_count * capacity
    pair_count = tok_rows * top_blocks
    centered = (tokens.astype(F32) - dec_bias).astype(BF16)
    owners = routes.reshape(pair_count)
    onehot = (owners[:, None] == jnp.arange(blk_count, dtype=jnp.int32)[None, :]).astype(jnp.int32)
    slot_rank = jnp.sum(jnp.cumsum(onehot, axis=0) * onehot, axis=1) - 1
    target = owners * capacity + slot_rank
    placing = jnp.arange(slot_count, dtype=jnp.int32)[:, None] == target[None, :]
    place_half = placing.astype(BF16)
    paired = jnp.repeat(centered, top_blocks, axis=0)
    outgoing = jnp.dot(place_half, paired, preferred_element_type=F32).astype(BF16)
    outgoing = outgoing.reshape(blk_count, capacity, quarter)
    sent_picks = jnp.dot(
        placing.astype(F32),
        latent_picks.reshape(pair_count, pick_count).astype(F32),
        precision=lax.Precision.HIGHEST,
    ).astype(jnp.int32)
    sent_picks = sent_picks.reshape(blk_count, capacity, pick_count)
    lat_ids = jnp.arange(latents, dtype=jnp.int32)
    arrived = lax.all_to_all(outgoing, "blocks", split_axis=0, concat_axis=0, tiled=True)
    chosen = lax.all_to_all(sent_picks, "blocks", split_axis=0, concat_axis=0, tiled=True)
    flat_rows = arrived.reshape(slot_count, quarter)
    chosen_ids = chosen.reshape(slot_count, pick_count)
    partial_value = jnp.dot(flat_rows, enc_weight[0], preferred_element_type=F32)
    summed = lax.psum(partial_value, "dp") + enc_bias[0][None, :]
    keep_mask = jnp.any(chosen_ids[:, :, None] == lat_ids[None, None, :], axis=1)
    active = jnp.where(keep_mask, jnp.maximum(summed, 0.0), 0.0).astype(BF16)
    partial_out = jnp.dot(active, dec_weight[0], preferred_element_type=F32).astype(BF16)
    partial_out = partial_out.reshape(blk_count, capacity, quarter)
    returned = lax.all_to_all(partial_out, "blocks", split_axis=0, concat_axis=0, tiled=True)
    back_rows = returned.reshape(slot_count, quarter)
    per_pair = jnp.einsum("sp,sd->pd", place_half, back_rows, preferred_element_type=F32)
    summed_out = per_pair.reshape(tok_rows, top_blocks, quarter).sum(axis=1) + dec_bias
    return summed_out.astype(BF16)


def outer_pairs(pairs):
    return [(a * INNER + i, b * INNER + i) for a, b in pairs for i in range(INNER)]


def inner_pairs(flip):
    return [(i, i ^ flip) for i in range(OUTER * INNER)]


ENDS = outer_pairs([(0, 1), (1, 0), (2, 3), (3, 2)])
MIDDLE = outer_pairs([(1, 2), (2, 1)])
OUTWARD = outer_pairs([(1, 0), (2, 3)])
INWARD = outer_pairs([(0, 1), (3, 2)])
FLIPS = {1: inner_pairs(1), 2: inner_pairs(2), 3: inner_pairs(3)}


def move(value, pairs):
    return lax.ppermute(value, "blocks", pairs)


def after(value, *others):
    return lax.optimization_barrier((value, *others))[0]


def call(kernel, name, grid, in_specs, out_specs, out_shape, scratch=()):
    return pl.pallas_call(
        kernel,
        name=name,
        grid=grid,
        in_specs=in_specs,
        out_specs=out_specs,
        out_shape=out_shape,
        scratch_shapes=scratch,
        compiler_params=pltpu.CompilerParams(vmem_limit_bytes=VMEM),
        cost_estimate=pl.CostEstimate(flops=0, bytes_accessed=0, transcendentals=0),
    )


def dispatch_kernel(cap, slots_ref, extra_refs, value_refs, offset_ref, spread_ref, out_refs, place_ref):
    rows = spread_ref.shape[0]

    @pl.when(pl.program_id(0) == 0)
    def _():
        extra = extra_refs[0][...].astype(F32)
        for ref in extra_refs[1:]:
            extra = extra + ref[...].astype(F32)
        hit = (extra[:, 0:1] == slots_ref[0:1, :]) | (extra[:, 1:2] == slots_ref[0:1, :])
        earlier = lax.broadcasted_iota(jnp.int32, (rows, rows), 1) < lax.broadcasted_iota(
            jnp.int32, (rows, rows), 0
        )
        rank = jnp.dot(
            jnp.where(earlier, 1.0, 0.0).astype(BF16),
            jnp.where(hit, 1.0, 0.0).astype(BF16),
            preferred_element_type=F32,
        )
        spread = jnp.where(hit & (rank == slots_ref[1:2, :]), 1.0, 0.0)
        spread_ref[...] = spread.astype(BF16)
        place_ref[...] = spread.T.astype(BF16)

    value = value_refs[0][...]
    for ref in value_refs[1:]:
        value = value + ref[...]
    moved = jnp.dot(place_ref[...], value, preferred_element_type=F32) - offset_ref[...]
    moved = moved.astype(BF16)
    for j, ref in enumerate(out_refs):
        ref[...] = moved[j * cap:(j + 1) * cap]


def dispatch(values, offset, slots, cap):
    rows, wide = values[0].shape
    step = wide // 3
    n = len(values)

    def kernel(slots_ref, *refs):
        dispatch_kernel(
            cap, slots_ref, refs[:n], refs[n:2 * n], refs[2 * n], refs[2 * n + 1], refs[2 * n + 2:-1], refs[-1]
        )

    spread, *pieces = call(
        kernel,
        "dispatch",
        (3,),
        [pl.BlockSpec((8, INNER * cap), lambda j: (0, 0))]
        + [pl.BlockSpec((rows, EXTRA), lambda j: (0, wide // EXTRA - 1))] * n
        + [pl.BlockSpec((rows, step), lambda j: (0, j))] * n
        + [pl.BlockSpec((1, step), lambda j: (0, j))],
        [pl.BlockSpec((rows, INNER * cap), lambda j: (0, 0))]
        + [pl.BlockSpec((cap, step), lambda j: (0, j))] * INNER,
        [jax.ShapeDtypeStruct((rows, INNER * cap), BF16)]
        + [jax.ShapeDtypeStruct((cap, wide), BF16)] * INNER,
        [pltpu.VMEM((INNER * cap, rows), BF16)],
    )(slots, *values, *values, offset)
    return spread, pieces


def encode_kernel(picked, piece_refs, extra_refs, enc_ref, bias_ref, me_ref, chosen_ref, picks_ref, total):
    k = pl.program_id(0)

    @pl.when(k == 0)
    def _():
        total[...] = jnp.broadcast_to(bias_ref[...], total.shape)

    mine = jnp.concatenate([ref[...] for ref in piece_refs], axis=0)
    total[...] += jnp.dot(mine, enc_ref[...], preferred_element_type=F32)

    @pl.when(k == pl.num_programs(0) - 1)
    def _():
        extra = jnp.concatenate([ref[...] for ref in extra_refs], axis=0).astype(F32)
        size = 2 * picked
        both = extra[:, 2:2 + size] * 32.0 + extra[:, 2 + size:2 + 2 * size]
        both = both.astype(jnp.int32)
        picks = jnp.where(extra[:, 0:1] == me_ref[0, 0], both[:, :picked], both[:, picked:])
        slots, latents = total.shape
        lane = lax.broadcasted_iota(jnp.int32, (slots, EXTRA), 1)
        ids = lax.broadcasted_iota(jnp.int32, (slots, latents), 1)
        values = jnp.zeros((slots, EXTRA), F32)
        kept = jnp.zeros((slots, EXTRA), jnp.int32)
        pre = total[...]
        for p in range(picked):
            pick = picks[:, p:p + 1]
            value = jnp.sum(jnp.where(ids == pick, pre, 0.0), axis=1, keepdims=True)
            values = jnp.where(lane == p, value, values)
            kept = jnp.where(lane == p, pick, kept)
        chosen_ref[...] = values.T[:picked]
        picks_ref[...] = kept


def encode(pieces, weight, bias, me, cap, picked):
    width, latents = weight.shape
    slots = INNER * cap
    last = width // EXTRA

    def kernel(*refs):
        encode_kernel(picked, refs[:INNER], refs[INNER:2 * INNER], *refs[2 * INNER:])

    return call(
        kernel,
        "encode",
        (width // BLOCK,),
        [pl.BlockSpec((cap, BLOCK), lambda k: (0, k))] * INNER
        + [pl.BlockSpec((cap, EXTRA), lambda k: (0, last))] * INNER
        + [
            pl.BlockSpec((BLOCK, latents), lambda k: (k, 0)),
            pl.BlockSpec((1, latents), lambda k: (0, 0)),
            pl.BlockSpec(memory_space=pltpu.SMEM),
        ],
        [
            pl.BlockSpec((picked, slots), lambda k: (0, 0)),
            pl.BlockSpec((slots, EXTRA), lambda k: (0, 0)),
        ],
        [
            jax.ShapeDtypeStruct((picked, slots), F32),
            jax.ShapeDtypeStruct((slots, EXTRA), jnp.int32),
        ],
        [pltpu.VMEM((slots, latents), F32)],
    )(*pieces, *pieces, weight, bias, me)


def decode_kernel(cap, chosen_ref, added_ref, picks_ref, dec_ref, *refs):
    active = refs[-1]

    @pl.when(pl.program_id(0) == 0)
    def _():
        picked, slots = chosen_ref.shape
        latents = active.shape[1]
        value = jnp.maximum(chosen_ref[...] + added_ref[...], 0.0)
        value = jnp.concatenate([value, jnp.zeros((EXTRA - picked, slots), F32)], axis=0).T
        ids = lax.broadcasted_iota(jnp.int32, (slots, latents), 1)
        dense = jnp.zeros((slots, latents), F32)
        for p in range(picked):
            dense = jnp.where(ids == picks_ref[:, p:p + 1], value[:, p:p + 1], dense)
        active[...] = dense.astype(BF16)

    part = jnp.dot(active[...], dec_ref[...], preferred_element_type=F32).astype(BF16)
    for j, ref in enumerate(refs[:-1]):
        ref[...] = part[j * cap:(j + 1) * cap]


def decode(chosen, added, picks, weight, cap, first, width):
    picked, slots = chosen.shape
    latents = weight.shape[0]
    skip = first // BLOCK
    return call(
        functools.partial(decode_kernel, cap),
        "decode",
        (width // BLOCK,),
        [
            pl.BlockSpec((picked, slots), lambda j: (0, 0)),
            pl.BlockSpec((picked, slots), lambda j: (0, 0)),
            pl.BlockSpec((slots, EXTRA), lambda j: (0, 0)),
            pl.BlockSpec((latents, BLOCK), lambda j: (0, j + skip)),
        ],
        [pl.BlockSpec((cap, BLOCK), lambda j: (0, j))] * INNER,
        [jax.ShapeDtypeStruct((cap, width), BF16)] * INNER,
        [pltpu.VMEM((slots, latents), BF16)],
    )(chosen, added, picks, weight)


def combine_kernel(spread_ref, *refs):
    parts = jnp.concatenate([ref[...] for ref in refs[:-1]], axis=0)
    refs[-1][...] = jnp.dot(spread_ref[...], parts, preferred_element_type=F32).astype(BF16)


def combine(spread, pieces, first, width):
    cap = pieces[0].shape[0]
    rows, slots = spread.shape
    step = min(width, 1024)
    skip = first // step
    return call(
        combine_kernel,
        "combine",
        (width // step,),
        [pl.BlockSpec((rows, slots), lambda j: (0, 0))]
        + [pl.BlockSpec((cap, step), lambda j: (0, j + skip))] * INNER,
        pl.BlockSpec((rows, step), lambda j: (0, j)),
        jax.ShapeDtypeStruct((rows, width), BF16),
    )(spread, *pieces)


def line_on_device(tokens, dec_bias, routes, latent_picks, enc_weight, dec_weight, enc_bias):
    rows, width = tokens.shape
    top = routes.shape[1]
    picked = latent_picks.shape[2]
    blk_count = lax.axis_size("blocks")
    cap = max(2, 2 * rows * top // blk_count)
    me = lax.axis_index("blocks")
    plane, inner = me // INNER, me % INNER

    flat_picks = latent_picks.reshape(rows, top * picked)
    meta = jnp.concatenate([routes, flat_picks // 32, flat_picks % 32], axis=1).astype(BF16)
    meta = jnp.pad(meta, ((0, 0), (0, EXTRA - meta.shape[1])))
    own = jnp.concatenate([tokens, meta], axis=1)
    offset = jnp.pad(dec_bias, (0, EXTRA))[None, :]
    slot = jnp.arange(INNER * cap, dtype=jnp.int32)
    slots = jnp.stack([plane * INNER + ((slot // cap) ^ inner), slot % cap]).astype(F32)
    slots = jnp.pad(slots, ((0, 6), (0, 0)))
    bias = jnp.where(lax.axis_index("dp") == 0, enc_bias, 0.0)
    me_value = me.astype(F32).reshape(1, 1)
    enc, dec = enc_weight[0], dec_weight[0]

    with jax.named_scope("rows_ends"):
        by_one = move(own, ENDS)
    with jax.named_scope("rows_middle"):
        by_two = move(own, MIDDLE)
    groups = {0: (own,)}

    def exchange(pieces, name):
        moved = [pieces[0]]
        for j in range(1, INNER):
            with jax.named_scope(f"{name}_{j}"):
                moved.append(move(pieces[j], FLIPS[j]))
        return moved

    def all_after(values, *earlier):
        values = tuple(values)
        return lax.optimization_barrier((*values, *earlier))[:len(values)]

    def send_out(t):
        spread, pieces = dispatch(groups[t], offset, slots, cap)
        return spread, exchange(pieces, f"out_{t}")

    def encoded(t, pieces):
        chosen, picks = encode(pieces, enc, bias, me_value, cap, picked)
        with jax.named_scope(f"sums_{t}"):
            added = lax.ppermute(chosen, "dp", [(0, 1), (1, 0)])
        return picks, chosen, added

    def decoded(t, picks, chosen, added):
        each = width // BACK_CHUNKS[t]
        return [
            decode(chosen, added, picks, dec, cap, i * each, each) for i in range(BACK_CHUNKS[t])
        ]

    def leave(t, parts, *earlier):
        if earlier:
            parts = [all_after(pieces, *earlier) for pieces in parts]
        return [exchange(pieces, f"back_{t}_{i}") for i, pieces in enumerate(parts)]

    def combined(spread, parts, count, *earlier):
        sums = []
        for pieces in parts:
            if earlier:
                pieces = all_after(pieces, *earlier)
            wide, each = pieces[0].shape[1], width // count
            for first in range(0, wide, each):
                sums.append(combine(spread, pieces, first, min(each, wide)))
        return sums

    def plus(a, b):
        return (a.astype(F32) + b.astype(F32)).astype(BF16)

    spreads, back = {}, {}
    spreads[0], arrived = send_out(0)
    waiting, returned = {}, {}
    for t in range(OUTER):
        if t > 0:
            arrived = all_after(arrived, *waiting[t - 1][0])
        if t > 1:
            returned[t - 1] = leave(t - 1, waiting[t - 1], *arrived[1:])
        picks, chosen, added = encoded(t, arrived)
        earlier = (chosen,)
        if t == 2:
            pieces = returned[1][0]
            pieces[2] = after(pieces[2], chosen)
            earlier = earlier + (pieces[2],)
        if t == 0:
            by_one, by_two = all_after((by_one, by_two), *earlier)
            with jax.named_scope("rows_outward_two"):
                to_ends_two = move(by_two, OUTWARD)
            with jax.named_scope("rows_middle_far"):
                by_three = move(by_one, MIDDLE)
            groups[1] = (by_one,)
        if t == 1:
            by_three, to_ends_two = all_after((by_three, to_ends_two), *earlier)
            with jax.named_scope("rows_outward_far"):
                to_ends_three = move(by_three, OUTWARD)
            groups[2] = (by_two, to_ends_two)
        if t == 2:
            groups[3] = (by_three, after(to_ends_three, *earlier))
        if t < OUTER - 1:
            spreads[t + 1], arrived = send_out(t + 1)
            added = after(added, spreads[t + 1])
        if t == 2:
            back[1] = combined(spreads[1], returned[1], 1, spreads[3])
            with jax.named_scope("sum_inward_one"):
                from_end = move(back[1][0], INWARD)
            added = after(added, *back[1])
        waiting[t] = decoded(t, picks, chosen, added)
    last = leave(3, waiting[3])
    back[2] = combined(spreads[2], returned[2], SUM_CHUNKS, *waiting[3][0])
    from_end = after(from_end, *back[2])
    back[3] = combined(spreads[3], last, SUM_CHUNKS, from_end)

    count = SUM_CHUNKS
    piece = width // count
    cols = [slice(i * piece, (i + 1) * piece) for i in range(count)]
    from_two, from_far = [], []
    for i in range(count):
        with jax.named_scope(f"sum_inward_two_{i}"):
            from_two.append(move(back[2][i], INWARD))
    for i in range(count):
        with jax.named_scope(f"sum_inward_far_{i}"):
            from_far.append(move(back[3][i], INWARD))
    twos, threes, ones, results = [], [], [], []
    seen = tuple(back[3])
    for i in range(count):
        got = after(from_two[i], *seen)
        with jax.named_scope(f"sum_middle_two_{i}"):
            twos.append(move(plus(back[2][i], got), MIDDLE))
        seen = (got,)
    for i in range(count):
        twos[i] = after(twos[i], *seen)
        got = after(from_far[i], twos[i])
        with jax.named_scope(f"sum_middle_far_{i}"):
            threes.append(move(plus(back[3][i], got), MIDDLE))
        seen = (got,)
    for i in range(count):
        got = after(threes[i], *seen)
        with jax.named_scope(f"sum_outward_far_{i}"):
            ones.append(move(plus(back[1][0][:, cols[i]], got), OUTWARD))
        seen = (ones[i],)
    returned[0] = leave(0, waiting[0], threes[0])
    back[0] = combined(spreads[0], returned[0], 1)
    for i in range(count):
        total = dec_bias[cols[i]]
        for value in (back[0][0][:, cols[i]], from_end[:, cols[i]], twos[i], ones[i]):
            total = total + value.astype(F32)
        results.append(total.astype(BF16))
    return jnp.concatenate(results, axis=1)


def solution(mesh):
    in_specs = (
        P("blocks", "dp"),
        P("dp"),
        P("blocks", None),
        P("blocks", None, None),
        P("blocks", "dp", None),
        P("blocks", None, "dp"),
        P("blocks", None),
    )
    on_device = line_on_device if mesh.shape["blocks"] == OUTER * INNER else flat_on_device
    return jax.shard_map(
        on_device, mesh=mesh, in_specs=in_specs, out_specs=P("blocks", "dp"), check_vma=False
    )
```

```python
import functools

import jax
import jax.numpy as jnp
from jax import lax
from jax.experimental import pallas as pl
from jax.experimental.pallas import tpu as pltpu
from jax.sharding import PartitionSpec as P

BACK_CHUNKS = (1, 1, 1, 1)
SUM_CHUNKS = 2
INNER = 4
OUTER = 4
EXTRA = 128
BLOCK = 512
VMEM = 24 * 1024 * 1024
F32 = jnp.float32
BF16 = jnp.bfloat16


def flat_on_device(tokens, dec_bias, routes, latent_picks, enc_weight, dec_weight, enc_bias):
    tok_rows, quarter = tokens.shape
    top_blocks = routes.shape[1]
    pick_count = latent_picks.shape[2]
    latents = enc_weight.shape[2]
    blk_count = lax.axis_size("blocks")
    capacity = max(2, 2 * tok_rows * top_blocks // blk_count)
    slot_count = blk_count * capacity
    pair_count = tok_rows * top_blocks
    centered = (tokens.astype(F32) - dec_bias).astype(BF16)
    owners = routes.reshape(pair_count)
    onehot = (owners[:, None] == jnp.arange(blk_count, dtype=jnp.int32)[None, :]).astype(jnp.int32)
    slot_rank = jnp.sum(jnp.cumsum(onehot, axis=0) * onehot, axis=1) - 1
    target = owners * capacity + slot_rank
    placing = jnp.arange(slot_count, dtype=jnp.int32)[:, None] == target[None, :]
    place_half = placing.astype(BF16)
    paired = jnp.repeat(centered, top_blocks, axis=0)
    outgoing = jnp.dot(place_half, paired, preferred_element_type=F32).astype(BF16)
    outgoing = outgoing.reshape(blk_count, capacity, quarter)
    sent_picks = jnp.dot(
        placing.astype(F32),
        latent_picks.reshape(pair_count, pick_count).astype(F32),
        precision=lax.Precision.HIGHEST,
    ).astype(jnp.int32)
    sent_picks = sent_picks.reshape(blk_count, capacity, pick_count)
    lat_ids = jnp.arange(latents, dtype=jnp.int32)
    arrived = lax.all_to_all(outgoing, "blocks", split_axis=0, concat_axis=0, tiled=True)
    chosen = lax.all_to_all(sent_picks, "blocks", split_axis=0, concat_axis=0, tiled=True)
    flat_rows = arrived.reshape(slot_count, quarter)
    chosen_ids = chosen.reshape(slot_count, pick_count)
    partial_value = jnp.dot(flat_rows, enc_weight[0], preferred_element_type=F32)
    summed = lax.psum(partial_value, "dp") + enc_bias[0][None, :]
    keep_mask = jnp.any(chosen_ids[:, :, None] == lat_ids[None, None, :], axis=1)
    active = jnp.where(keep_mask, jnp.maximum(summed, 0.0), 0.0).astype(BF16)
    partial_out = jnp.dot(active, dec_weight[0], preferred_element_type=F32).astype(BF16)
    partial_out = partial_out.reshape(blk_count, capacity, quarter)
    returned = lax.all_to_all(partial_out, "blocks", split_axis=0, concat_axis=0, tiled=True)
    back_rows = returned.reshape(slot_count, quarter)
    per_pair = jnp.einsum("sp,sd->pd", place_half, back_rows, preferred_element_type=F32)
    summed_out = per_pair.reshape(tok_rows, top_blocks, quarter).sum(axis=1) + dec_bias
    return summed_out.astype(BF16)


def outer_pairs(pairs):
    return [(a * INNER + i, b * INNER + i) for a, b in pairs for i in range(INNER)]


def inner_pairs(flip):
    return [(i, i ^ flip) for i in range(OUTER * INNER)]


ENDS = outer_pairs([(0, 1), (1, 0), (2, 3), (3, 2)])
MIDDLE = outer_pairs([(1, 2), (2, 1)])
OUTWARD = outer_pairs([(1, 0), (2, 3)])
INWARD = outer_pairs([(0, 1), (3, 2)])
SKIP = outer_pairs([(1, 3), (2, 0)])
FLIPS = {1: inner_pairs(1), 2: inner_pairs(2), 3: inner_pairs(3)}


def move(value, pairs):
    return lax.ppermute(value, "blocks", pairs)


def after(value, *others):
    return lax.optimization_barrier((value, *others))[0]


def call(kernel, name, grid, in_specs, out_specs, out_shape, scratch=()):
    return pl.pallas_call(
        kernel,
        name=name,
        grid=grid,
        in_specs=in_specs,
        out_specs=out_specs,
        out_shape=out_shape,
        scratch_shapes=scratch,
        compiler_params=pltpu.CompilerParams(vmem_limit_bytes=VMEM),
        cost_estimate=pl.CostEstimate(flops=0, bytes_accessed=0, transcendentals=0),
    )


def dispatch_kernel(cap, slots_ref, extra_refs, value_refs, offset_ref, spread_ref, out_refs, place_ref):
    rows = spread_ref.shape[0]

    @pl.when(pl.program_id(0) == 0)
    def _():
        extra = extra_refs[0][...].astype(F32)
        for ref in extra_refs[1:]:
            extra = extra + ref[...].astype(F32)
        hit = (extra[:, 0:1] == slots_ref[0:1, :]) | (extra[:, 1:2] == slots_ref[0:1, :])
        earlier = lax.broadcasted_iota(jnp.int32, (rows, rows), 1) < lax.broadcasted_iota(
            jnp.int32, (rows, rows), 0
        )
        rank = jnp.dot(
            jnp.where(earlier, 1.0, 0.0).astype(BF16),
            jnp.where(hit, 1.0, 0.0).astype(BF16),
            preferred_element_type=F32,
        )
        spread = jnp.where(hit & (rank == slots_ref[1:2, :]), 1.0, 0.0)
        spread_ref[...] = spread.astype(BF16)
        place_ref[...] = spread.T.astype(BF16)

    value = value_refs[0][...]
    for ref in value_refs[1:]:
        value = value + ref[...]
    moved = jnp.dot(place_ref[...], value, preferred_element_type=F32) - offset_ref[...]
    moved = moved.astype(BF16)
    for j, ref in enumerate(out_refs):
        ref[...] = moved[j * cap:(j + 1) * cap]


def dispatch(values, offset, slots, cap):
    rows, wide = values[0].shape
    step = wide // 3
    n = len(values)

    def kernel(slots_ref, *refs):
        dispatch_kernel(
            cap, slots_ref, refs[:n], refs[n:2 * n], refs[2 * n], refs[2 * n + 1], refs[2 * n + 2:-1], refs[-1]
        )

    spread, *pieces = call(
        kernel,
        "dispatch",
        (3,),
        [pl.BlockSpec((8, INNER * cap), lambda j: (0, 0))]
        + [pl.BlockSpec((rows, EXTRA), lambda j: (0, wide // EXTRA - 1))] * n
        + [pl.BlockSpec((rows, step), lambda j: (0, j))] * n
        + [pl.BlockSpec((1, step), lambda j: (0, j))],
        [pl.BlockSpec((rows, INNER * cap), lambda j: (0, 0))]
        + [pl.BlockSpec((cap, step), lambda j: (0, j))] * INNER,
        [jax.ShapeDtypeStruct((rows, INNER * cap), BF16)]
        + [jax.ShapeDtypeStruct((cap, wide), BF16)] * INNER,
        [pltpu.VMEM((INNER * cap, rows), BF16)],
    )(slots, *values, *values, offset)
    return spread, pieces


def encode_kernel(picked, piece_refs, extra_refs, enc_ref, bias_ref, me_ref, chosen_ref, picks_ref, total):
    k = pl.program_id(0)

    @pl.when(k == 0)
    def _():
        total[...] = jnp.broadcast_to(bias_ref[...], total.shape)

    mine = jnp.concatenate([ref[...] for ref in piece_refs], axis=0)
    total[...] += jnp.dot(mine, enc_ref[...], preferred_element_type=F32)

    @pl.when(k == pl.num_programs(0) - 1)
    def _():
        extra = jnp.concatenate([ref[...] for ref in extra_refs], axis=0).astype(F32)
        size = 2 * picked
        both = extra[:, 2:2 + size] * 32.0 + extra[:, 2 + size:2 + 2 * size]
        both = both.astype(jnp.int32)
        picks = jnp.where(extra[:, 0:1] == me_ref[0, 0], both[:, :picked], both[:, picked:])
        slots, latents = total.shape
        lane = lax.broadcasted_iota(jnp.int32, (slots, EXTRA), 1)
        ids = lax.broadcasted_iota(jnp.int32, (slots, latents), 1)
        values = jnp.zeros((slots, EXTRA), F32)
        kept = jnp.zeros((slots, EXTRA), jnp.int32)
        pre = total[...]
        for p in range(picked):
            pick = picks[:, p:p + 1]
            value = jnp.sum(jnp.where(ids == pick, pre, 0.0), axis=1, keepdims=True)
            values = jnp.where(lane == p, value, values)
            kept = jnp.where(lane == p, pick, kept)
        chosen_ref[...] = values.T[:picked]
        picks_ref[...] = kept


def encode(pieces, weight, bias, me, cap, picked):
    width, latents = weight.shape
    slots = INNER * cap
    last = width // EXTRA

    def kernel(*refs):
        encode_kernel(picked, refs[:INNER], refs[INNER:2 * INNER], *refs[2 * INNER:])

    return call(
        kernel,
        "encode",
        (width // BLOCK,),
        [pl.BlockSpec((cap, BLOCK), lambda k: (0, k))] * INNER
        + [pl.BlockSpec((cap, EXTRA), lambda k: (0, last))] * INNER
        + [
            pl.BlockSpec((BLOCK, latents), lambda k: (k, 0)),
            pl.BlockSpec((1, latents), lambda k: (0, 0)),
            pl.BlockSpec(memory_space=pltpu.SMEM),
        ],
        [
            pl.BlockSpec((picked, slots), lambda k: (0, 0)),
            pl.BlockSpec((slots, EXTRA), lambda k: (0, 0)),
        ],
        [
            jax.ShapeDtypeStruct((picked, slots), F32),
            jax.ShapeDtypeStruct((slots, EXTRA), jnp.int32),
        ],
        [pltpu.VMEM((slots, latents), F32)],
    )(*pieces, *pieces, weight, bias, me)


def decode_kernel(cap, chosen_ref, added_ref, picks_ref, dec_ref, *refs):
    active = refs[-1]

    @pl.when(pl.program_id(0) == 0)
    def _():
        picked, slots = chosen_ref.shape
        latents = active.shape[1]
        value = jnp.maximum(chosen_ref[...] + added_ref[...], 0.0)
        value = jnp.concatenate([value, jnp.zeros((EXTRA - picked, slots), F32)], axis=0).T
        ids = lax.broadcasted_iota(jnp.int32, (slots, latents), 1)
        dense = jnp.zeros((slots, latents), F32)
        for p in range(picked):
            dense = jnp.where(ids == picks_ref[:, p:p + 1], value[:, p:p + 1], dense)
        active[...] = dense.astype(BF16)

    part = jnp.dot(active[...], dec_ref[...], preferred_element_type=F32).astype(BF16)
    for j, ref in enumerate(refs[:-1]):
        ref[...] = part[j * cap:(j + 1) * cap]


def decode(chosen, added, picks, weight, cap, first, width):
    picked, slots = chosen.shape
    latents = weight.shape[0]
    skip = first // BLOCK
    return call(
        functools.partial(decode_kernel, cap),
        "decode",
        (width // BLOCK,),
        [
            pl.BlockSpec((picked, slots), lambda j: (0, 0)),
            pl.BlockSpec((picked, slots), lambda j: (0, 0)),
            pl.BlockSpec((slots, EXTRA), lambda j: (0, 0)),
            pl.BlockSpec((latents, BLOCK), lambda j: (0, j + skip)),
        ],
        [pl.BlockSpec((cap, BLOCK), lambda j: (0, j))] * INNER,
        [jax.ShapeDtypeStruct((cap, width), BF16)] * INNER,
        [pltpu.VMEM((slots, latents), BF16)],
    )(chosen, added, picks, weight)


def combine_kernel(spread_ref, *refs):
    parts = jnp.concatenate([ref[...] for ref in refs[:-1]], axis=0)
    refs[-1][...] = jnp.dot(spread_ref[...], parts, preferred_element_type=F32).astype(BF16)


def combine(spread, pieces, first, width):
    cap = pieces[0].shape[0]
    rows, slots = spread.shape
    step = min(width, 1024)
    skip = first // step
    return call(
        combine_kernel,
        "combine",
        (width // step,),
        [pl.BlockSpec((rows, slots), lambda j: (0, 0))]
        + [pl.BlockSpec((cap, step), lambda j: (0, j + skip))] * INNER,
        pl.BlockSpec((rows, step), lambda j: (0, j)),
        jax.ShapeDtypeStruct((rows, width), BF16),
    )(spread, *pieces)


def line_on_device(tokens, dec_bias, routes, latent_picks, enc_weight, dec_weight, enc_bias):
    rows, width = tokens.shape
    top = routes.shape[1]
    picked = latent_picks.shape[2]
    blk_count = lax.axis_size("blocks")
    cap = max(2, 2 * rows * top // blk_count)
    me = lax.axis_index("blocks")
    plane, inner = me // INNER, me % INNER

    flat_picks = latent_picks.reshape(rows, top * picked)
    meta = jnp.concatenate([routes, flat_picks // 32, flat_picks % 32], axis=1).astype(BF16)
    meta = jnp.pad(meta, ((0, 0), (0, EXTRA - meta.shape[1])))
    own = jnp.concatenate([tokens, meta], axis=1)
    offset = jnp.pad(dec_bias, (0, EXTRA))[None, :]
    slot = jnp.arange(INNER * cap, dtype=jnp.int32)
    slots = jnp.stack([plane * INNER + ((slot // cap) ^ inner), slot % cap]).astype(F32)
    slots = jnp.pad(slots, ((0, 6), (0, 0)))
    bias = jnp.where(lax.axis_index("dp") == 0, enc_bias, 0.0)
    me_value = me.astype(F32).reshape(1, 1)
    enc, dec = enc_weight[0], dec_weight[0]

    with jax.named_scope("rows_ends"):
        by_one = move(own, ENDS)
    with jax.named_scope("rows_middle"):
        by_two = move(own, MIDDLE)
    groups = {0: (own,)}

    def exchange(pieces, name):
        moved = [pieces[0]]
        for j in range(1, INNER):
            with jax.named_scope(f"{name}_{j}"):
                moved.append(move(pieces[j], FLIPS[j]))
        return moved

    def all_after(values, *earlier):
        values = tuple(values)
        return lax.optimization_barrier((*values, *earlier))[:len(values)]

    def send_out(t):
        spread, pieces = dispatch(groups[t], offset, slots, cap)
        return spread, exchange(pieces, f"out_{t}")

    def encoded(t, pieces):
        chosen, picks = encode(pieces, enc, bias, me_value, cap, picked)
        with jax.named_scope(f"sums_{t}"):
            added = lax.ppermute(chosen, "dp", [(0, 1), (1, 0)])
        return picks, chosen, added

    def decoded(t, picks, chosen, added):
        each = width // BACK_CHUNKS[t]
        return [
            decode(chosen, added, picks, dec, cap, i * each, each) for i in range(BACK_CHUNKS[t])
        ]

    def leave(t, parts, *earlier):
        if earlier:
            parts = [all_after(pieces, *earlier) for pieces in parts]
        return [exchange(pieces, f"back_{t}_{i}") for i, pieces in enumerate(parts)]

    def combined(spread, parts, count, *earlier):
        sums = []
        for pieces in parts:
            if earlier:
                pieces = all_after(pieces, *earlier)
            wide, each = pieces[0].shape[1], width // count
            for first in range(0, wide, each):
                sums.append(combine(spread, pieces, first, min(each, wide)))
        return sums

    def plus(a, b):
        return (a.astype(F32) + b.astype(F32)).astype(BF16)

    spreads, back = {}, {}
    spreads[0], arrived = send_out(0)
    waiting, returned = {}, {}
    for t in range(OUTER):
        if t > 0:
            arrived = all_after(arrived, *waiting[t - 1][0])
        if t > 1:
            returned[t - 1] = leave(t - 1, waiting[t - 1], *arrived[1:])
        picks, chosen, added = encoded(t, arrived)
        earlier = (chosen,)
        if t == 2:
            pieces = returned[1][0]
            pieces[2] = after(pieces[2], chosen)
            earlier = earlier + (pieces[2],)
        if t == 0:
            by_one, by_two = all_after((by_one, by_two), *earlier)
            with jax.named_scope("rows_outward_two"):
                to_ends_two = move(by_two, OUTWARD)
            with jax.named_scope("rows_middle_far"):
                by_three = move(by_one, MIDDLE)
            groups[1] = (by_one,)
        if t == 1:
            by_three, to_ends_two = all_after((by_three, to_ends_two), *earlier)
            with jax.named_scope("rows_outward_far"):
                to_ends_three = move(by_three, OUTWARD)
            groups[2] = (by_two, to_ends_two)
        if t == 2:
            groups[3] = (by_three, after(to_ends_three, *earlier))
        if t < OUTER - 1:
            spreads[t + 1], arrived = send_out(t + 1)
            added = after(added, spreads[t + 1])
        if t == 2:
            back[1] = combined(spreads[1], returned[1], 1, spreads[3])
            with jax.named_scope("sum_ends"):
                from_end = move(back[1][0], ENDS)
            added = after(added, *back[1])
        waiting[t] = decoded(t, picks, chosen, added)
    last = leave(3, waiting[3])
    back[2] = combined(spreads[2], returned[2], SUM_CHUNKS, *waiting[3][0])
    from_end = after(from_end, *back[2])
    back[3] = combined(spreads[3], last, SUM_CHUNKS, from_end)

    count = SUM_CHUNKS
    piece = width // count
    cols = [slice(i * piece, (i + 1) * piece) for i in range(count)]
    from_two, from_far = [], []
    for i in range(count):
        with jax.named_scope(f"sum_inward_two_{i}"):
            from_two.append(move(back[2][i], INWARD))
    for i in range(count):
        with jax.named_scope(f"sum_inward_far_{i}"):
            from_far.append(move(back[3][i], INWARD))
    twos, ones, results = [], [], []
    seen = tuple(back[3])
    for i in range(count):
        got = after(from_two[i], *seen)
        with jax.named_scope(f"sum_middle_two_{i}"):
            twos.append(move(plus(back[2][i], got), MIDDLE))
        seen = (got,)
    for i in range(count):
        twos[i] = after(twos[i], *seen)
        if i == 0:
            returned[0] = leave(0, waiting[0], twos[0])
            got = after(from_far[i], twos[i])
        else:
            pieces = returned[0][0]
            pieces[2] = after(pieces[2], twos[i])
            got = after(from_far[i], pieces[2], ones[i - 1])
        with jax.named_scope(f"sum_skip_far_{i}"):
            ones.append(move(plus(back[3][i], got), SKIP))
        seen = (got,)
    back[0] = combined(spreads[0], returned[0], 1, *seen)
    ones[-1] = after(ones[-1], *back[0])
    for i in range(count):
        total = dec_bias[cols[i]]
        for value in (back[0][0][:, cols[i]], from_end[:, cols[i]], twos[i], ones[i]):
            total = total + value.astype(F32)
        results.append(total.astype(BF16))
    return jnp.concatenate(results, axis=1)


def solution(mesh):
    in_specs = (
        P("blocks", "dp"),
        P("dp"),
        P("blocks", None),
        P("blocks", None, None),
        P("blocks", "dp", None),
        P("blocks", None, "dp"),
        P("blocks", None),
    )
    on_device = line_on_device if mesh.shape["blocks"] == OUTER * INNER else flat_on_device
    return jax.shard_map(
        on_device, mesh=mesh, in_specs=in_specs, out_specs=P("blocks", "dp"), check_vma=False
    )
```

```python
import functools
import math

import jax
import jax.numpy as jnp
from jax import lax
from jax.experimental import pallas as pl
from jax.experimental.pallas import tpu as pltpu
from jax.sharding import PartitionSpec as P

BACK_CHUNKS = (1, 1, 1, 1)
TWO_SHARES = (1, 1)
FAR_SHARES = (1, 1)
INNER = 4
OUTER = 4
EXTRA = 128
BLOCK = 1024
VMEM = 24 * 1024 * 1024
F32 = jnp.float32
BF16 = jnp.bfloat16


def flat_on_device(tokens, dec_bias, routes, latent_picks, enc_weight, dec_weight, enc_bias):
    tok_rows, quarter = tokens.shape
    top_blocks = routes.shape[1]
    pick_count = latent_picks.shape[2]
    latents = enc_weight.shape[2]
    blk_count = lax.axis_size("blocks")
    capacity = max(2, 2 * tok_rows * top_blocks // blk_count)
    slot_count = blk_count * capacity
    pair_count = tok_rows * top_blocks
    centered = (tokens.astype(F32) - dec_bias).astype(BF16)
    owners = routes.reshape(pair_count)
    onehot = (owners[:, None] == jnp.arange(blk_count, dtype=jnp.int32)[None, :]).astype(jnp.int32)
    slot_rank = jnp.sum(jnp.cumsum(onehot, axis=0) * onehot, axis=1) - 1
    target = owners * capacity + slot_rank
    placing = jnp.arange(slot_count, dtype=jnp.int32)[:, None] == target[None, :]
    place_half = placing.astype(BF16)
    paired = jnp.repeat(centered, top_blocks, axis=0)
    outgoing = jnp.dot(place_half, paired, preferred_element_type=F32).astype(BF16)
    outgoing = outgoing.reshape(blk_count, capacity, quarter)
    sent_picks = jnp.dot(
        placing.astype(F32),
        latent_picks.reshape(pair_count, pick_count).astype(F32),
        precision=lax.Precision.HIGHEST,
    ).astype(jnp.int32)
    sent_picks = sent_picks.reshape(blk_count, capacity, pick_count)
    lat_ids = jnp.arange(latents, dtype=jnp.int32)
    arrived = lax.all_to_all(outgoing, "blocks", split_axis=0, concat_axis=0, tiled=True)
    chosen = lax.all_to_all(sent_picks, "blocks", split_axis=0, concat_axis=0, tiled=True)
    flat_rows = arrived.reshape(slot_count, quarter)
    chosen_ids = chosen.reshape(slot_count, pick_count)
    partial_value = jnp.dot(flat_rows, enc_weight[0], preferred_element_type=F32)
    summed = lax.psum(partial_value, "dp") + enc_bias[0][None, :]
    keep_mask = jnp.any(chosen_ids[:, :, None] == lat_ids[None, None, :], axis=1)
    active = jnp.where(keep_mask, jnp.maximum(summed, 0.0), 0.0).astype(BF16)
    partial_out = jnp.dot(active, dec_weight[0], preferred_element_type=F32).astype(BF16)
    partial_out = partial_out.reshape(blk_count, capacity, quarter)
    returned = lax.all_to_all(partial_out, "blocks", split_axis=0, concat_axis=0, tiled=True)
    back_rows = returned.reshape(slot_count, quarter)
    per_pair = jnp.einsum("sp,sd->pd", place_half, back_rows, preferred_element_type=F32)
    summed_out = per_pair.reshape(tok_rows, top_blocks, quarter).sum(axis=1) + dec_bias
    return summed_out.astype(BF16)


def outer_pairs(pairs):
    return [(a * INNER + i, b * INNER + i) for a, b in pairs for i in range(INNER)]


def inner_pairs(flip):
    return [(i, i ^ flip) for i in range(OUTER * INNER)]


ENDS = outer_pairs([(0, 1), (1, 0), (2, 3), (3, 2)])
MIDDLE = outer_pairs([(1, 2), (2, 1)])
OUTWARD = outer_pairs([(1, 0), (2, 3)])
INWARD = outer_pairs([(0, 1), (3, 2)])
SKIP = outer_pairs([(1, 3), (2, 0)])
FLIPS = {1: inner_pairs(1), 2: inner_pairs(2), 3: inner_pairs(3)}


def move(value, pairs):
    return lax.ppermute(value, "blocks", pairs)


def after(value, *others):
    return lax.optimization_barrier((value, *others))[0]


def call(kernel, name, grid, in_specs, out_specs, out_shape, scratch=()):
    return pl.pallas_call(
        kernel,
        name=name,
        grid=grid,
        in_specs=in_specs,
        out_specs=out_specs,
        out_shape=out_shape,
        scratch_shapes=scratch,
        compiler_params=pltpu.CompilerParams(vmem_limit_bytes=VMEM),
        cost_estimate=pl.CostEstimate(flops=0, bytes_accessed=0, transcendentals=0),
    )


def dispatch_kernel(cap, slots_ref, extra_refs, value_refs, offset_ref, spread_ref, out_refs, place_ref):
    rows = spread_ref.shape[0]

    @pl.when(pl.program_id(0) == 0)
    def _():
        extra = extra_refs[0][...].astype(F32)
        for ref in extra_refs[1:]:
            extra = extra + ref[...].astype(F32)
        hit = (extra[:, 0:1] == slots_ref[0:1, :]) | (extra[:, 1:2] == slots_ref[0:1, :])
        earlier = lax.broadcasted_iota(jnp.int32, (rows, rows), 1) < lax.broadcasted_iota(
            jnp.int32, (rows, rows), 0
        )
        rank = jnp.dot(
            jnp.where(earlier, 1.0, 0.0).astype(BF16),
            jnp.where(hit, 1.0, 0.0).astype(BF16),
            preferred_element_type=F32,
        )
        spread = jnp.where(hit & (rank == slots_ref[1:2, :]), 1.0, 0.0)
        spread_ref[...] = spread.astype(BF16)
        place_ref[...] = spread.T.astype(BF16)

    value = value_refs[0][...]
    for ref in value_refs[1:]:
        value = value + ref[...]
    moved = jnp.dot(place_ref[...], value, preferred_element_type=F32) - offset_ref[...]
    moved = moved.astype(BF16)
    for j, ref in enumerate(out_refs):
        ref[...] = moved[j * cap:(j + 1) * cap]


def dispatch(values, offset, slots, cap):
    rows, wide = values[0].shape
    step = wide // 3
    n = len(values)

    def kernel(slots_ref, *refs):
        dispatch_kernel(
            cap, slots_ref, refs[:n], refs[n:2 * n], refs[2 * n], refs[2 * n + 1], refs[2 * n + 2:-1], refs[-1]
        )

    spread, *pieces = call(
        kernel,
        "dispatch",
        (3,),
        [pl.BlockSpec((8, INNER * cap), lambda j: (0, 0))]
        + [pl.BlockSpec((rows, EXTRA), lambda j: (0, wide // EXTRA - 1))] * n
        + [pl.BlockSpec((rows, step), lambda j: (0, j))] * n
        + [pl.BlockSpec((1, step), lambda j: (0, j))],
        [pl.BlockSpec((rows, INNER * cap), lambda j: (0, 0))]
        + [pl.BlockSpec((cap, step), lambda j: (0, j))] * INNER,
        [jax.ShapeDtypeStruct((rows, INNER * cap), BF16)]
        + [jax.ShapeDtypeStruct((cap, wide), BF16)] * INNER,
        [pltpu.VMEM((INNER * cap, rows), BF16)],
    )(slots, *values, *values, offset)
    return spread, pieces


def encode_kernel(picked, piece_refs, extra_refs, enc_ref, bias_ref, me_ref, chosen_ref, picks_ref, total):
    k = pl.program_id(0)

    @pl.when(k == 0)
    def _():
        total[...] = jnp.broadcast_to(bias_ref[...], total.shape)

    mine = jnp.concatenate([ref[...] for ref in piece_refs], axis=0)
    total[...] += jnp.dot(mine, enc_ref[...], preferred_element_type=F32)

    @pl.when(k == pl.num_programs(0) - 1)
    def _():
        extra = jnp.concatenate([ref[...] for ref in extra_refs], axis=0).astype(F32)
        size = 2 * picked
        both = extra[:, 2:2 + size] * 32.0 + extra[:, 2 + size:2 + 2 * size]
        both = both.astype(jnp.int32)
        picks = jnp.where(extra[:, 0:1] == me_ref[0, 0], both[:, :picked], both[:, picked:])
        slots, latents = total.shape
        picks = jnp.concatenate([picks, jnp.zeros((slots, EXTRA - picked), jnp.int32)], axis=1)
        group, lane = picks // EXTRA, picks % EXTRA
        values = jnp.zeros((slots, EXTRA), F32)
        for g in range(latents // EXTRA):
            here = total[:, g * EXTRA:(g + 1) * EXTRA]
            values = jnp.where(group == g, jnp.take_along_axis(here, lane, axis=1), values)
        chosen_ref[...] = values.T[:picked]
        picks_ref[...] = picks.astype(F32).T[:picked].astype(jnp.int32)


def encode(pieces, weight, bias, me, cap, picked):
    width, latents = weight.shape
    slots = INNER * cap
    last = width // EXTRA

    def kernel(*refs):
        encode_kernel(picked, refs[:INNER], refs[INNER:2 * INNER], *refs[2 * INNER:])

    return call(
        kernel,
        "encode",
        (width // BLOCK,),
        [pl.BlockSpec((cap, BLOCK), lambda k: (0, k))] * INNER
        + [pl.BlockSpec((cap, EXTRA), lambda k: (0, last))] * INNER
        + [
            pl.BlockSpec((BLOCK, latents), lambda k: (k, 0)),
            pl.BlockSpec((1, latents), lambda k: (0, 0)),
            pl.BlockSpec(memory_space=pltpu.SMEM),
        ],
        [
            pl.BlockSpec((picked, slots), lambda k: (0, 0)),
            pl.BlockSpec((picked, slots), lambda k: (0, 0)),
        ],
        [
            jax.ShapeDtypeStruct((picked, slots), F32),
            jax.ShapeDtypeStruct((picked, slots), jnp.int32),
        ],
        [pltpu.VMEM((slots, latents), F32)],
    )(*pieces, *pieces, weight, bias, me)


def decode_kernel(chosen_ref, added_ref, picks_ref, dec_ref, *refs):
    active = refs[-1]

    @pl.when(pl.program_id(0) == 0)
    def _():
        picked, slots = chosen_ref.shape
        latents = active.shape[1]
        value = jnp.maximum(chosen_ref[...] + added_ref[...], 0.0)
        ids = lax.broadcasted_iota(jnp.int32, (latents, slots), 0)
        dense = jnp.zeros((latents, slots), F32)
        for p in range(picked):
            dense = jnp.where(ids == picks_ref[p:p + 1, :], value[p:p + 1, :], dense)
        active[...] = dense.T.astype(BF16)

    part = jnp.dot(active[...], dec_ref[...], preferred_element_type=F32).astype(BF16)
    first = 0
    for ref in refs[:-1]:
        ref[...] = part[first:first + ref.shape[0]]
        first += ref.shape[0]


def decode(chosen, added, picks, weight, sizes):
    picked, slots = chosen.shape
    latents, width = weight.shape
    return call(
        decode_kernel,
        "decode",
        (width // BLOCK,),
        [
            pl.BlockSpec((picked, slots), lambda j: (0, 0)),
            pl.BlockSpec((picked, slots), lambda j: (0, 0)),
            pl.BlockSpec((picked, slots), lambda j: (0, 0)),
            pl.BlockSpec((latents, BLOCK), lambda j: (0, j)),
        ],
        [pl.BlockSpec((size, BLOCK), lambda j: (0, j)) for size in sizes],
        [jax.ShapeDtypeStruct((size, width), BF16) for size in sizes],
        [pltpu.VMEM((slots, latents), BF16)],
    )(chosen, added, picks, weight)


def combine_kernel(spread_ref, *refs):
    parts = jnp.concatenate([ref[...] for ref in refs[:-1]], axis=0)
    total = jnp.dot(spread_ref[...], parts, preferred_element_type=F32)
    refs[-1][...] = total.astype(refs[-1].dtype)


def combine(spread, blocks, cap, first, width, dtype=BF16):
    rows, slots = spread.shape
    step = math.gcd(math.gcd(first, width), 1024)
    skip = first // step
    return call(
        combine_kernel,
        "combine",
        (width // step,),
        [pl.BlockSpec((rows, slots), lambda j: (0, 0))]
        + [pl.BlockSpec((cap, step), lambda j, at=at: (at, j + skip)) for _, at in blocks],
        pl.BlockSpec((rows, step), lambda j: (0, j)),
        jax.ShapeDtypeStruct((rows, width), dtype),
    )(spread, *(array for array, _ in blocks))


def spread_kernel(slots_ref, meta_ref, spread_ref):
    rows = spread_ref.shape[0]
    extra = meta_ref[...].astype(F32)
    hit = (extra[:, 0:1] == slots_ref[0:1, :]) | (extra[:, 1:2] == slots_ref[0:1, :])
    earlier = lax.broadcasted_iota(jnp.int32, (rows, rows), 1) < lax.broadcasted_iota(
        jnp.int32, (rows, rows), 0
    )
    rank = jnp.dot(
        jnp.where(earlier, 1.0, 0.0).astype(BF16),
        jnp.where(hit, 1.0, 0.0).astype(BF16),
        preferred_element_type=F32,
    )
    spread = jnp.where(hit & (rank == slots_ref[1:2, :]), 1.0, 0.0)
    spread_ref[...] = spread.astype(BF16)


def spread_of(slots, meta):
    return call(
        spread_kernel,
        "spread",
        (),
        [pl.BlockSpec(memory_space=pltpu.VMEM)] * 2,
        pl.BlockSpec(memory_space=pltpu.VMEM),
        jax.ShapeDtypeStruct((meta.shape[0], slots.shape[1]), BF16),
    )(slots, meta)


def line_on_device(tokens, dec_bias, routes, latent_picks, enc_weight, dec_weight, enc_bias):
    rows, width = tokens.shape
    top = routes.shape[1]
    picked = latent_picks.shape[2]
    blk_count = lax.axis_size("blocks")
    cap = max(2, 2 * rows * top // blk_count)
    me = lax.axis_index("blocks")
    plane, inner = me // INNER, me % INNER

    flat_picks = latent_picks.reshape(rows, top * picked)
    meta = jnp.concatenate([routes, flat_picks // 32, flat_picks % 32], axis=1).astype(BF16)
    meta = jnp.pad(meta, ((0, 0), (0, EXTRA - meta.shape[1])))
    own = jnp.concatenate([tokens, meta], axis=1)
    offset = jnp.pad(dec_bias, (0, EXTRA))[None, :]
    slot = jnp.arange(INNER * cap, dtype=jnp.int32)

    def slots_in(which):
        named = jnp.stack([which * INNER + ((slot // cap) ^ inner), slot % cap]).astype(F32)
        return jnp.pad(named, ((0, 6), (0, 0)))

    slots = slots_in(plane)
    bias = jnp.where(lax.axis_index("dp") == 0, enc_bias, 0.0)
    me_value = me.astype(F32).reshape(1, 1)
    enc, dec = enc_weight[0], dec_weight[0]

    with jax.named_scope("rows_ends"):
        by_one = move(own, ENDS)
    with jax.named_scope("rows_middle"):
        by_two = move(own, MIDDLE)
    groups = {0: (own,)}

    def exchange(pieces, name):
        moved = [pieces[0]]
        for j in range(1, INNER):
            with jax.named_scope(f"{name}_{j}"):
                moved.append(move(pieces[j], FLIPS[j]))
        return moved

    def all_after(values, *earlier):
        values = tuple(values)
        return lax.optimization_barrier((*values, *earlier))[:len(values)]

    def send_out(t):
        spread, pieces = dispatch(groups[t], offset, slots, cap)
        return spread, exchange(pieces, f"out_{t}")

    def encoded(t, pieces):
        chosen, picks = encode(pieces, enc, bias, me_value, cap, picked)
        with jax.named_scope(f"sums_{t}"):
            added = lax.ppermute(chosen, "dp", [(0, 1), (1, 0)])
        return picks, chosen, added

    def decoded(picks, chosen, added, sizes=(cap,) * INNER):
        return decode(chosen, added, picks, dec, sizes)

    def leave(t, pieces):
        return exchange(pieces, f"back_{t}")

    def combined(spread, pieces, shares):
        sums, first = [], 0
        for share in shares:
            size = width * share // sum(shares)
            sums.append(combine(spread, [(piece, 0) for piece in pieces], cap, first, size))
            first += size
        return sums

    def plus(a, b):
        return (a.astype(F32) + b.astype(F32)).astype(BF16)

    spreads, parts = {}, {}
    spreads[0], arrived = send_out(0)
    spread_next = spread_of(slots_in(plane ^ 1), meta)

    picks, chosen, added = encoded(0, arrived)
    added = after(added, chosen)
    by_one, by_two = all_after((by_one, by_two), added)
    with jax.named_scope("rows_outward_two"):
        to_ends_two = move(by_two, OUTWARD)
    with jax.named_scope("rows_middle_far"):
        by_three = move(by_one, MIDDLE)
    groups[1] = (by_one,)
    spreads[1], arrived = send_out(1)
    parts[0] = decoded(picks, chosen, after(added, spreads[1]))

    picks, chosen, added = encoded(1, all_after(arrived, *parts[0]))
    (parts1,) = decoded(picks, chosen, added, (INNER * cap,))
    with jax.named_scope("parts_inward"):
        inward = move(parts1, INWARD)
    to_ends_two = after(to_ends_two, parts1)
    by_three = after(by_three, to_ends_two)
    with jax.named_scope("rows_outward_far"):
        to_ends_three = move(by_three, OUTWARD)
    groups[2] = (by_two, to_ends_two)
    spreads[2], arrived = send_out(2)

    picks, chosen, added = encoded(2, arrived)
    parts[2] = decoded(picks, chosen, added)
    returned2 = leave(2, parts[2])
    to_ends_three = after(to_ends_three, *parts[2])
    returned2[1] = after(returned2[1], to_ends_three)
    with jax.named_scope("parts_outward"):
        outward = move(after(parts1, to_ends_three), OUTWARD)
    groups[3] = (by_three, after(to_ends_three, returned2[1]))
    spreads[3], arrived = send_out(3)
    arrived[1] = after(arrived[1], spreads[3])
    arrived[2] = after(arrived[2], arrived[1])
    inward = after(inward, arrived[2])
    arrived[3] = after(arrived[3], inward)

    picks, chosen, added = encoded(3, arrived)
    parts[3] = decoded(picks, chosen, added)
    returned3 = leave(3, parts[3])
    back2 = combined(spreads[2], all_after(returned2, *parts[3]), TWO_SHARES)
    from_two = []
    for i, value in enumerate(back2):
        with jax.named_scope(f"sum_inward_two_{i}"):
            from_two.append(move(value, INWARD))
    twos, ones = [], []

    def two_on(i, *earlier):
        from_two[i] = after(from_two[i], *earlier)
        with jax.named_scope(f"sum_middle_two_{i}"):
            twos.append(move(plus(back2[i], from_two[i]), MIDDLE))

    returned3[2] = after(returned3[2], *back2)
    two_on(0, returned3[2])
    returned3 = all_after(returned3, from_two[0])
    back3 = combined(spreads[3], returned3, FAR_SHARES)
    two_on(1, *back3)
    twos[0] = after(twos[0], from_two[1])
    outward = after(outward, from_two[1])
    from_far = []
    for i, value in enumerate(back3):
        with jax.named_scope(f"sum_inward_far_{i}"):
            from_far.append(move(value, INWARD))

    near = inward + outward
    pieces = []
    for j in range(1, INNER):
        pieces.append(jnp.concatenate([parts[0][j], near[j * cap:(j + 1) * cap]], axis=0))
    pieces = exchange([None, *all_after(pieces, *returned3)], "back_near")

    def skip_on(i, *earlier):
        from_far[i] = after(from_far[i], *earlier)
        with jax.named_scope(f"sum_skip_far_{i}"):
            ones.append(move(plus(back3[i], from_far[i]), SKIP))

    skip_on(0, pieces[2], twos[0])
    twos[1] = after(twos[1], from_far[0])
    pieces[3] = after(pieces[3], twos[1])
    skip_on(1, pieces[3], ones[0])
    pieces[1] = after(pieces[1], from_far[1])
    blocks = [(parts[0][0], 0)] + [(piece, 0) for piece in pieces[1:]]
    blocks += [(near, 0)] + [(piece, 1) for piece in pieces[1:]]
    near = combine(
        jnp.concatenate([spreads[0], spread_next], axis=1), blocks, cap, 0, width, F32
    )
    ones = all_after(ones, near)
    near = near + dec_bias + jnp.concatenate(twos, axis=1).astype(F32)
    return (near + jnp.concatenate(ones, axis=1).astype(F32)).astype(BF16)


def solution(mesh):
    in_specs = (
        P("blocks", "dp"),
        P("dp"),
        P("blocks", None),
        P("blocks", None, None),
        P("blocks", "dp", None),
        P("blocks", None, "dp"),
        P("blocks", None),
    )
    on_device = line_on_device if mesh.shape["blocks"] == OUTER * INNER else flat_on_device
    return jax.shard_map(
        on_device, mesh=mesh, in_specs=in_specs, out_specs=P("blocks", "dp"), check_vma=False
    )
```

```python
import functools
import math

import jax
import jax.numpy as jnp
from jax import lax
from jax.experimental import pallas as pl
from jax.experimental.pallas import tpu as pltpu
from jax.sharding import PartitionSpec as P

BACK_CHUNKS = (1, 1, 1, 1)
TWO_SHARES = (1, 1)
FAR_SHARES = (1, 1)
INNER = 4
OUTER = 4
EXTRA = 128
BLOCK = 1024
VMEM = 24 * 1024 * 1024
F32 = jnp.float32
BF16 = jnp.bfloat16


def flat_on_device(tokens, dec_bias, routes, latent_picks, enc_weight, dec_weight, enc_bias):
    tok_rows, quarter = tokens.shape
    top_blocks = routes.shape[1]
    pick_count = latent_picks.shape[2]
    latents = enc_weight.shape[2]
    blk_count = lax.axis_size("blocks")
    capacity = max(2, 2 * tok_rows * top_blocks // blk_count)
    slot_count = blk_count * capacity
    pair_count = tok_rows * top_blocks
    centered = (tokens.astype(F32) - dec_bias).astype(BF16)
    owners = routes.reshape(pair_count)
    onehot = (owners[:, None] == jnp.arange(blk_count, dtype=jnp.int32)[None, :]).astype(jnp.int32)
    slot_rank = jnp.sum(jnp.cumsum(onehot, axis=0) * onehot, axis=1) - 1
    target = owners * capacity + slot_rank
    placing = jnp.arange(slot_count, dtype=jnp.int32)[:, None] == target[None, :]
    place_half = placing.astype(BF16)
    paired = jnp.repeat(centered, top_blocks, axis=0)
    outgoing = jnp.dot(place_half, paired, preferred_element_type=F32).astype(BF16)
    outgoing = outgoing.reshape(blk_count, capacity, quarter)
    sent_picks = jnp.dot(
        placing.astype(F32),
        latent_picks.reshape(pair_count, pick_count).astype(F32),
        precision=lax.Precision.HIGHEST,
    ).astype(jnp.int32)
    sent_picks = sent_picks.reshape(blk_count, capacity, pick_count)
    lat_ids = jnp.arange(latents, dtype=jnp.int32)
    arrived = lax.all_to_all(outgoing, "blocks", split_axis=0, concat_axis=0, tiled=True)
    chosen = lax.all_to_all(sent_picks, "blocks", split_axis=0, concat_axis=0, tiled=True)
    flat_rows = arrived.reshape(slot_count, quarter)
    chosen_ids = chosen.reshape(slot_count, pick_count)
    partial_value = jnp.dot(flat_rows, enc_weight[0], preferred_element_type=F32)
    summed = lax.psum(partial_value, "dp") + enc_bias[0][None, :]
    keep_mask = jnp.any(chosen_ids[:, :, None] == lat_ids[None, None, :], axis=1)
    active = jnp.where(keep_mask, jnp.maximum(summed, 0.0), 0.0).astype(BF16)
    partial_out = jnp.dot(active, dec_weight[0], preferred_element_type=F32).astype(BF16)
    partial_out = partial_out.reshape(blk_count, capacity, quarter)
    returned = lax.all_to_all(partial_out, "blocks", split_axis=0, concat_axis=0, tiled=True)
    back_rows = returned.reshape(slot_count, quarter)
    per_pair = jnp.einsum("sp,sd->pd", place_half, back_rows, preferred_element_type=F32)
    summed_out = per_pair.reshape(tok_rows, top_blocks, quarter).sum(axis=1) + dec_bias
    return summed_out.astype(BF16)


def outer_pairs(pairs):
    return [(a * INNER + i, b * INNER + i) for a, b in pairs for i in range(INNER)]


def inner_pairs(flip):
    return [(i, i ^ flip) for i in range(OUTER * INNER)]


ENDS = outer_pairs([(0, 1), (1, 0), (2, 3), (3, 2)])
MIDDLE = outer_pairs([(1, 2), (2, 1)])
OUTWARD = outer_pairs([(1, 0), (2, 3)])
INWARD = outer_pairs([(0, 1), (3, 2)])
SKIP = outer_pairs([(1, 3), (2, 0)])
FLIPS = {1: inner_pairs(1), 2: inner_pairs(2), 3: inner_pairs(3)}


def move(value, pairs):
    return lax.ppermute(value, "blocks", pairs)


def after(value, *others):
    return lax.optimization_barrier((value, *others))[0]


def call(kernel, name, grid, in_specs, out_specs, out_shape, scratch=()):
    return pl.pallas_call(
        kernel,
        name=name,
        grid=grid,
        in_specs=in_specs,
        out_specs=out_specs,
        out_shape=out_shape,
        scratch_shapes=scratch,
        compiler_params=pltpu.CompilerParams(vmem_limit_bytes=VMEM),
        cost_estimate=pl.CostEstimate(flops=0, bytes_accessed=0, transcendentals=0),
    )


def dispatch_kernel(cap, n, slots_ref, offset_ref, *refs):
    value_refs, (spread_ref, *out_refs) = refs[:n], refs[n:]
    rows, wide = value_refs[0].shape
    extra = value_refs[0][:, wide - EXTRA:].astype(F32)
    for ref in value_refs[1:]:
        extra = extra + ref[:, wide - EXTRA:].astype(F32)
    hit = (extra[:, 0:1] == slots_ref[0:1, :]) | (extra[:, 1:2] == slots_ref[0:1, :])
    earlier = lax.broadcasted_iota(jnp.int32, (rows, rows), 1) < lax.broadcasted_iota(
        jnp.int32, (rows, rows), 0
    )
    rank = jnp.dot(
        jnp.where(earlier, 1.0, 0.0).astype(BF16),
        jnp.where(hit, 1.0, 0.0).astype(BF16),
        preferred_element_type=F32,
    )
    spread = jnp.where(hit & (rank == slots_ref[1:2, :]), 1.0, 0.0)
    spread_ref[...] = spread.astype(BF16)
    value = value_refs[0][...]
    for ref in value_refs[1:]:
        value = value + ref[...]
    place = spread.T.astype(BF16)
    moved = (jnp.dot(place, value, preferred_element_type=F32) - offset_ref[...]).astype(BF16)
    for j, ref in enumerate(out_refs):
        ref[...] = moved[j * cap:(j + 1) * cap]


def dispatch(values, offset, slots, cap):
    rows, wide = values[0].shape
    spread, *pieces = call(
        functools.partial(dispatch_kernel, cap, len(values)),
        "dispatch",
        (),
        [pl.BlockSpec(memory_space=pltpu.VMEM)] * (2 + len(values)),
        [pl.BlockSpec(memory_space=pltpu.VMEM)] * (1 + INNER),
        [jax.ShapeDtypeStruct((rows, INNER * cap), BF16)]
        + [jax.ShapeDtypeStruct((cap, wide), BF16)] * INNER,
    )(slots, offset, *values)
    return spread, pieces


def encode_kernel(picked, piece_refs, extra_refs, enc_ref, bias_ref, me_ref, chosen_ref, picks_ref, total):
    k = pl.program_id(0)

    @pl.when(k == 0)
    def _():
        total[...] = jnp.broadcast_to(bias_ref[...], total.shape)

    mine = jnp.concatenate([ref[...] for ref in piece_refs], axis=0)
    total[...] += jnp.dot(mine, enc_ref[...], preferred_element_type=F32)

    @pl.when(k == pl.num_programs(0) - 1)
    def _():
        extra = jnp.concatenate([ref[...] for ref in extra_refs], axis=0).astype(F32)
        size = 2 * picked
        both = extra[:, 2:2 + size] * 32.0 + extra[:, 2 + size:2 + 2 * size]
        both = both.astype(jnp.int32)
        picks = jnp.where(extra[:, 0:1] == me_ref[0, 0], both[:, :picked], both[:, picked:])
        slots, latents = total.shape
        picks = jnp.concatenate([picks, jnp.zeros((slots, EXTRA - picked), jnp.int32)], axis=1)
        group, lane = picks // EXTRA, picks % EXTRA
        values = jnp.zeros((slots, EXTRA), F32)
        for g in range(latents // EXTRA):
            here = total[:, g * EXTRA:(g + 1) * EXTRA]
            values = jnp.where(group == g, jnp.take_along_axis(here, lane, axis=1), values)
        chosen_ref[...] = values.T[:picked]
        picks_ref[...] = picks.astype(F32).T[:picked].astype(jnp.int32)


def encode(pieces, weight, bias, me, cap, picked):
    width, latents = weight.shape
    slots = INNER * cap
    last = width // EXTRA

    def kernel(*refs):
        encode_kernel(picked, refs[:INNER], refs[INNER:2 * INNER], *refs[2 * INNER:])

    return call(
        kernel,
        "encode",
        (width // BLOCK,),
        [pl.BlockSpec((cap, BLOCK), lambda k: (0, k))] * INNER
        + [pl.BlockSpec((cap, EXTRA), lambda k: (0, last))] * INNER
        + [
            pl.BlockSpec((BLOCK, latents), lambda k: (k, 0)),
            pl.BlockSpec((1, latents), lambda k: (0, 0)),
            pl.BlockSpec(memory_space=pltpu.SMEM),
        ],
        [
            pl.BlockSpec((picked, slots), lambda k: (0, 0)),
            pl.BlockSpec((picked, slots), lambda k: (0, 0)),
        ],
        [
            jax.ShapeDtypeStruct((picked, slots), F32),
            jax.ShapeDtypeStruct((picked, slots), jnp.int32),
        ],
        [pltpu.VMEM((slots, latents), F32)],
    )(*pieces, *pieces, weight, bias, me)


def decode_kernel(chosen_ref, added_ref, picks_ref, dec_ref, *refs):
    active = refs[-1]

    @pl.when(pl.program_id(0) == 0)
    def _():
        picked, slots = chosen_ref.shape
        latents = active.shape[1]
        value = jnp.maximum(chosen_ref[...] + added_ref[...], 0.0)
        ids = lax.broadcasted_iota(jnp.int32, (latents, slots), 0)
        dense = jnp.zeros((latents, slots), F32)
        for p in range(picked):
            dense = jnp.where(ids == picks_ref[p:p + 1, :], value[p:p + 1, :], dense)
        active[...] = dense.T.astype(BF16)

    part = jnp.dot(active[...], dec_ref[...], preferred_element_type=F32).astype(BF16)
    first = 0
    for ref in refs[:-1]:
        ref[...] = part[first:first + ref.shape[0]]
        first += ref.shape[0]


def decode(chosen, added, picks, weight, sizes):
    picked, slots = chosen.shape
    latents, width = weight.shape
    return call(
        decode_kernel,
        "decode",
        (width // BLOCK,),
        [
            pl.BlockSpec((picked, slots), lambda j: (0, 0)),
            pl.BlockSpec((picked, slots), lambda j: (0, 0)),
            pl.BlockSpec((picked, slots), lambda j: (0, 0)),
            pl.BlockSpec((latents, BLOCK), lambda j: (0, j)),
        ],
        [pl.BlockSpec((size, BLOCK), lambda j: (0, j)) for size in sizes],
        [jax.ShapeDtypeStruct((size, width), BF16) for size in sizes],
        [pltpu.VMEM((slots, latents), BF16)],
    )(chosen, added, picks, weight)


def combine_kernel(spread_ref, *refs):
    parts = jnp.concatenate([ref[...] for ref in refs[:-1]], axis=0)
    total = jnp.dot(spread_ref[...], parts, preferred_element_type=F32)
    refs[-1][...] = total.astype(refs[-1].dtype)


def combine(spread, blocks, cap, first, width, dtype=BF16):
    rows, slots = spread.shape
    step = math.gcd(math.gcd(first, width), 1024)
    skip = first // step
    return call(
        combine_kernel,
        "combine",
        (width // step,),
        [pl.BlockSpec((rows, slots), lambda j: (0, 0))]
        + [pl.BlockSpec((cap, step), lambda j, at=at: (at, j + skip)) for _, at in blocks],
        pl.BlockSpec((rows, step), lambda j: (0, j)),
        jax.ShapeDtypeStruct((rows, width), dtype),
    )(spread, *(array for array, _ in blocks))


def spread_kernel(slots_ref, meta_ref, spread_ref):
    rows = spread_ref.shape[0]
    extra = meta_ref[...].astype(F32)
    hit = (extra[:, 0:1] == slots_ref[0:1, :]) | (extra[:, 1:2] == slots_ref[0:1, :])
    earlier = lax.broadcasted_iota(jnp.int32, (rows, rows), 1) < lax.broadcasted_iota(
        jnp.int32, (rows, rows), 0
    )
    rank = jnp.dot(
        jnp.where(earlier, 1.0, 0.0).astype(BF16),
        jnp.where(hit, 1.0, 0.0).astype(BF16),
        preferred_element_type=F32,
    )
    spread = jnp.where(hit & (rank == slots_ref[1:2, :]), 1.0, 0.0)
    spread_ref[...] = spread.astype(BF16)


def spread_of(slots, meta):
    return call(
        spread_kernel,
        "spread",
        (),
        [pl.BlockSpec(memory_space=pltpu.VMEM)] * 2,
        pl.BlockSpec(memory_space=pltpu.VMEM),
        jax.ShapeDtypeStruct((meta.shape[0], slots.shape[1]), BF16),
    )(slots, meta)


def line_on_device(tokens, dec_bias, routes, latent_picks, enc_weight, dec_weight, enc_bias):
    rows, width = tokens.shape
    top = routes.shape[1]
    picked = latent_picks.shape[2]
    blk_count = lax.axis_size("blocks")
    cap = max(2, 2 * rows * top // blk_count)
    me = lax.axis_index("blocks")
    plane, inner = me // INNER, me % INNER

    flat_picks = latent_picks.reshape(rows, top * picked)
    meta = jnp.concatenate([routes, flat_picks // 32, flat_picks % 32], axis=1).astype(BF16)
    meta = jnp.pad(meta, ((0, 0), (0, EXTRA - meta.shape[1])))
    own = jnp.concatenate([tokens, meta], axis=1)
    offset = jnp.pad(dec_bias, (0, EXTRA))[None, :]
    slot = jnp.arange(INNER * cap, dtype=jnp.int32)

    def slots_in(which):
        named = jnp.stack([which * INNER + ((slot // cap) ^ inner), slot % cap]).astype(F32)
        return jnp.pad(named, ((0, 6), (0, 0)))

    slots = slots_in(plane)
    bias = jnp.where(lax.axis_index("dp") == 0, enc_bias, 0.0)
    me_value = me.astype(F32).reshape(1, 1)
    enc, dec = enc_weight[0], dec_weight[0]

    with jax.named_scope("rows_ends"):
        by_one = move(own, ENDS)
    with jax.named_scope("rows_middle"):
        by_two = move(own, MIDDLE)
    groups = {0: (own,)}

    def exchange(pieces, name):
        moved = [pieces[0]]
        for j in range(1, INNER):
            with jax.named_scope(f"{name}_{j}"):
                moved.append(move(pieces[j], FLIPS[j]))
        return moved

    def all_after(values, *earlier):
        values = tuple(values)
        return lax.optimization_barrier((*values, *earlier))[:len(values)]

    def send_out(t):
        spread, pieces = dispatch(groups[t], offset, slots, cap)
        return spread, exchange(pieces, f"out_{t}")

    def encoded(t, pieces):
        chosen, picks = encode(pieces, enc, bias, me_value, cap, picked)
        with jax.named_scope(f"sums_{t}"):
            added = lax.ppermute(chosen, "dp", [(0, 1), (1, 0)])
        return picks, chosen, added

    def decoded(picks, chosen, added, sizes=(cap,) * INNER):
        return decode(chosen, added, picks, dec, sizes)

    def leave(t, pieces):
        return exchange(pieces, f"back_{t}")

    def combined(spread, pieces, shares):
        sums, first = [], 0
        for share in shares:
            size = width * share // sum(shares)
            sums.append(combine(spread, [(piece, 0) for piece in pieces], cap, first, size))
            first += size
        return sums

    def plus(a, b):
        return (a.astype(F32) + b.astype(F32)).astype(BF16)

    spreads, parts = {}, {}
    spreads[0], arrived = send_out(0)
    spread_next = spread_of(slots_in(plane ^ 1), meta)

    picks, chosen, added = encoded(0, arrived)
    added = after(added, chosen)
    by_one, by_two = all_after((by_one, by_two), added)
    with jax.named_scope("rows_outward_two"):
        to_ends_two = move(by_two, OUTWARD)
    with jax.named_scope("rows_middle_far"):
        by_three = move(by_one, MIDDLE)
    groups[1] = (by_one,)
    spreads[1], arrived = send_out(1)
    parts[0] = decoded(picks, chosen, after(added, spreads[1]))

    picks, chosen, added = encoded(1, all_after(arrived, *parts[0]))
    (parts1,) = decoded(picks, chosen, added, (INNER * cap,))
    with jax.named_scope("parts_inward"):
        inward = move(parts1, INWARD)
    to_ends_two = after(to_ends_two, parts1)
    by_three = after(by_three, to_ends_two)
    with jax.named_scope("rows_outward_far"):
        to_ends_three = move(by_three, OUTWARD)
    groups[2] = (by_two, to_ends_two)
    spreads[2], arrived = send_out(2)

    picks, chosen, added = encoded(2, arrived)
    parts[2] = decoded(picks, chosen, added)
    returned2 = leave(2, parts[2])
    to_ends_three = after(to_ends_three, *parts[2])
    returned2[1] = after(returned2[1], to_ends_three)
    with jax.named_scope("parts_outward"):
        outward = move(after(parts1, to_ends_three), OUTWARD)
    groups[3] = (by_three, after(to_ends_three, returned2[1]))
    spreads[3], arrived = send_out(3)
    arrived[1] = after(arrived[1], spreads[3])
    arrived[2] = after(arrived[2], arrived[1])
    inward = after(inward, arrived[2])
    arrived[3] = after(arrived[3], inward)

    picks, chosen, added = encoded(3, arrived)
    parts[3] = decoded(picks, chosen, added)
    returned3 = leave(3, parts[3])
    back2 = combined(spreads[2], all_after(returned2, *parts[3]), TWO_SHARES)
    from_two = []
    for i, value in enumerate(back2):
        with jax.named_scope(f"sum_inward_two_{i}"):
            from_two.append(move(value, INWARD))
    twos, ones = [], []

    def two_on(i, *earlier):
        from_two[i] = after(from_two[i], *earlier)
        with jax.named_scope(f"sum_middle_two_{i}"):
            twos.append(move(plus(back2[i], from_two[i]), MIDDLE))

    returned3[2] = after(returned3[2], *back2)
    outward = after(outward, returned3[2])
    two_on(0, outward)
    returned3 = all_after(returned3, from_two[0])
    back3 = combined(spreads[3], returned3, FAR_SHARES)
    two_on(1, *back3)
    twos[0] = after(twos[0], from_two[1])
    from_far = []
    for i, value in enumerate(back3):
        with jax.named_scope(f"sum_inward_far_{i}"):
            from_far.append(move(value, INWARD))

    near = inward + outward
    pieces = []
    for j in range(1, INNER):
        pieces.append(jnp.concatenate([parts[0][j], near[j * cap:(j + 1) * cap]], axis=0))
    pieces = exchange([None, *all_after(pieces, *returned3)], "back_near")

    def skip_on(i, *earlier):
        from_far[i] = after(from_far[i], *earlier)
        with jax.named_scope(f"sum_skip_far_{i}"):
            ones.append(move(plus(back3[i], from_far[i]), SKIP))

    skip_on(0, pieces[2], twos[0])
    twos[1] = after(twos[1], from_far[0])
    pieces[3] = after(pieces[3], twos[1])
    skip_on(1, pieces[3], ones[0])
    pieces[1] = after(pieces[1], from_far[1])
    blocks = [(parts[0][0], 0)] + [(piece, 0) for piece in pieces[1:]]
    blocks += [(near, 0)] + [(piece, 1) for piece in pieces[1:]]
    near = combine(
        jnp.concatenate([spreads[0], spread_next], axis=1), blocks, cap, 0, width, F32
    )
    ones = all_after(ones, near)
    near = near + dec_bias + jnp.concatenate(twos, axis=1).astype(F32)
    return (near + jnp.concatenate(ones, axis=1).astype(F32)).astype(BF16)


def solution(mesh):
    in_specs = (
        P("blocks", "dp"),
        P("dp"),
        P("blocks", None),
        P("blocks", None, None),
        P("blocks", "dp", None),
        P("blocks", None, "dp"),
        P("blocks", None),
    )
    on_device = line_on_device if mesh.shape["blocks"] == OUTER * INNER else flat_on_device
    return jax.shard_map(
        on_device, mesh=mesh, in_specs=in_specs, out_specs=P("blocks", "dp"), check_vma=False
    )
```

```python
import functools
import math

import jax
import jax.numpy as jnp
from jax import lax
from jax.experimental import pallas as pl
from jax.experimental.pallas import tpu as pltpu
from jax.sharding import PartitionSpec as P

BACK_CHUNKS = (1, 1, 1, 1)
TWO_SHARES = (1, 1)
FAR_SHARES = (3, 5)
INNER = 4
OUTER = 4
EXTRA = 128
BLOCK = 1024
VMEM = 24 * 1024 * 1024
F32 = jnp.float32
BF16 = jnp.bfloat16


def flat_on_device(tokens, dec_bias, routes, latent_picks, enc_weight, dec_weight, enc_bias):
    tok_rows, quarter = tokens.shape
    top_blocks = routes.shape[1]
    pick_count = latent_picks.shape[2]
    latents = enc_weight.shape[2]
    blk_count = lax.axis_size("blocks")
    capacity = max(2, 2 * tok_rows * top_blocks // blk_count)
    slot_count = blk_count * capacity
    pair_count = tok_rows * top_blocks
    centered = (tokens.astype(F32) - dec_bias).astype(BF16)
    owners = routes.reshape(pair_count)
    onehot = (owners[:, None] == jnp.arange(blk_count, dtype=jnp.int32)[None, :]).astype(jnp.int32)
    slot_rank = jnp.sum(jnp.cumsum(onehot, axis=0) * onehot, axis=1) - 1
    target = owners * capacity + slot_rank
    placing = jnp.arange(slot_count, dtype=jnp.int32)[:, None] == target[None, :]
    place_half = placing.astype(BF16)
    paired = jnp.repeat(centered, top_blocks, axis=0)
    outgoing = jnp.dot(place_half, paired, preferred_element_type=F32).astype(BF16)
    outgoing = outgoing.reshape(blk_count, capacity, quarter)
    sent_picks = jnp.dot(
        placing.astype(F32),
        latent_picks.reshape(pair_count, pick_count).astype(F32),
        precision=lax.Precision.HIGHEST,
    ).astype(jnp.int32)
    sent_picks = sent_picks.reshape(blk_count, capacity, pick_count)
    lat_ids = jnp.arange(latents, dtype=jnp.int32)
    arrived = lax.all_to_all(outgoing, "blocks", split_axis=0, concat_axis=0, tiled=True)
    chosen = lax.all_to_all(sent_picks, "blocks", split_axis=0, concat_axis=0, tiled=True)
    flat_rows = arrived.reshape(slot_count, quarter)
    chosen_ids = chosen.reshape(slot_count, pick_count)
    partial_value = jnp.dot(flat_rows, enc_weight[0], preferred_element_type=F32)
    summed = lax.psum(partial_value, "dp") + enc_bias[0][None, :]
    keep_mask = jnp.any(chosen_ids[:, :, None] == lat_ids[None, None, :], axis=1)
    active = jnp.where(keep_mask, jnp.maximum(summed, 0.0), 0.0).astype(BF16)
    partial_out = jnp.dot(active, dec_weight[0], preferred_element_type=F32).astype(BF16)
    partial_out = partial_out.reshape(blk_count, capacity, quarter)
    returned = lax.all_to_all(partial_out, "blocks", split_axis=0, concat_axis=0, tiled=True)
    back_rows = returned.reshape(slot_count, quarter)
    per_pair = jnp.einsum("sp,sd->pd", place_half, back_rows, preferred_element_type=F32)
    summed_out = per_pair.reshape(tok_rows, top_blocks, quarter).sum(axis=1) + dec_bias
    return summed_out.astype(BF16)


def outer_pairs(pairs):
    return [(a * INNER + i, b * INNER + i) for a, b in pairs for i in range(INNER)]


def inner_pairs(flip):
    return [(i, i ^ flip) for i in range(OUTER * INNER)]


ENDS = outer_pairs([(0, 1), (1, 0), (2, 3), (3, 2)])
MIDDLE = outer_pairs([(1, 2), (2, 1)])
OUTWARD = outer_pairs([(1, 0), (2, 3)])
INWARD = outer_pairs([(0, 1), (3, 2)])
SKIP = outer_pairs([(1, 3), (2, 0)])
FLIPS = {1: inner_pairs(1), 2: inner_pairs(2), 3: inner_pairs(3)}


def move(value, pairs):
    return lax.ppermute(value, "blocks", pairs)


def after(value, *others):
    return lax.optimization_barrier((value, *others))[0]


def call(kernel, name, grid, in_specs, out_specs, out_shape, scratch=()):
    return pl.pallas_call(
        kernel,
        name=name,
        grid=grid,
        in_specs=in_specs,
        out_specs=out_specs,
        out_shape=out_shape,
        scratch_shapes=scratch,
        compiler_params=pltpu.CompilerParams(vmem_limit_bytes=VMEM),
        cost_estimate=pl.CostEstimate(flops=0, bytes_accessed=0, transcendentals=0),
    )


def dispatch_kernel(cap, n, slots_ref, offset_ref, *refs):
    value_refs, (spread_ref, *out_refs) = refs[:n], refs[n:]
    rows, wide = value_refs[0].shape
    extra = value_refs[0][:, wide - EXTRA:].astype(F32)
    for ref in value_refs[1:]:
        extra = extra + ref[:, wide - EXTRA:].astype(F32)
    hit = (extra[:, 0:1] == slots_ref[0:1, :]) | (extra[:, 1:2] == slots_ref[0:1, :])
    earlier = lax.broadcasted_iota(jnp.int32, (rows, rows), 1) < lax.broadcasted_iota(
        jnp.int32, (rows, rows), 0
    )
    rank = jnp.dot(
        jnp.where(earlier, 1.0, 0.0).astype(BF16),
        jnp.where(hit, 1.0, 0.0).astype(BF16),
        preferred_element_type=F32,
    )
    spread = jnp.where(hit & (rank == slots_ref[1:2, :]), 1.0, 0.0)
    spread_ref[...] = spread.astype(BF16)
    value = value_refs[0][...]
    for ref in value_refs[1:]:
        value = value + ref[...]
    place = spread.T.astype(BF16)
    moved = (jnp.dot(place, value, preferred_element_type=F32) - offset_ref[...]).astype(BF16)
    for j, ref in enumerate(out_refs):
        ref[...] = moved[j * cap:(j + 1) * cap]


def dispatch(values, offset, slots, cap):
    rows, wide = values[0].shape
    spread, *pieces = call(
        functools.partial(dispatch_kernel, cap, len(values)),
        "dispatch",
        (),
        [pl.BlockSpec(memory_space=pltpu.VMEM)] * (2 + len(values)),
        [pl.BlockSpec(memory_space=pltpu.VMEM)] * (1 + INNER),
        [jax.ShapeDtypeStruct((rows, INNER * cap), BF16)]
        + [jax.ShapeDtypeStruct((cap, wide), BF16)] * INNER,
    )(slots, offset, *values)
    return spread, pieces


def encode_kernel(picked, piece_refs, extra_refs, enc_ref, bias_ref, me_ref, chosen_ref, picks_ref, total):
    k = pl.program_id(0)

    @pl.when(k == 0)
    def _():
        total[...] = jnp.broadcast_to(bias_ref[...], total.shape)

    mine = jnp.concatenate([ref[...] for ref in piece_refs], axis=0)
    total[...] += jnp.dot(mine, enc_ref[...], preferred_element_type=F32)

    @pl.when(k == pl.num_programs(0) - 1)
    def _():
        extra = jnp.concatenate([ref[...] for ref in extra_refs], axis=0).astype(F32)
        size = 2 * picked
        both = extra[:, 2:2 + size] * 32.0 + extra[:, 2 + size:2 + 2 * size]
        both = both.astype(jnp.int32)
        picks = jnp.where(extra[:, 0:1] == me_ref[0, 0], both[:, :picked], both[:, picked:])
        slots, latents = total.shape
        picks = jnp.concatenate([picks, jnp.zeros((slots, EXTRA - picked), jnp.int32)], axis=1)
        group, lane = picks // EXTRA, picks % EXTRA
        values = jnp.zeros((slots, EXTRA), F32)
        for g in range(latents // EXTRA):
            here = total[:, g * EXTRA:(g + 1) * EXTRA]
            values = jnp.where(group == g, jnp.take_along_axis(here, lane, axis=1), values)
        chosen_ref[...] = values.T[:picked]
        picks_ref[...] = picks.astype(F32).T[:picked].astype(jnp.int32)


def encode(pieces, weight, bias, me, cap, picked):
    width, latents = weight.shape
    slots = INNER * cap
    last = width // EXTRA

    def kernel(*refs):
        encode_kernel(picked, refs[:INNER], refs[INNER:2 * INNER], *refs[2 * INNER:])

    return call(
        kernel,
        "encode",
        (width // BLOCK,),
        [pl.BlockSpec((cap, BLOCK), lambda k: (0, k))] * INNER
        + [pl.BlockSpec((cap, EXTRA), lambda k: (0, last))] * INNER
        + [
            pl.BlockSpec((BLOCK, latents), lambda k: (k, 0)),
            pl.BlockSpec((1, latents), lambda k: (0, 0)),
            pl.BlockSpec(memory_space=pltpu.SMEM),
        ],
        [
            pl.BlockSpec((picked, slots), lambda k: (0, 0)),
            pl.BlockSpec((picked, slots), lambda k: (0, 0)),
        ],
        [
            jax.ShapeDtypeStruct((picked, slots), F32),
            jax.ShapeDtypeStruct((picked, slots), jnp.int32),
        ],
        [pltpu.VMEM((slots, latents), F32)],
    )(*pieces, *pieces, weight, bias, me)


def decode_kernel(chosen_ref, added_ref, picks_ref, dec_ref, *refs):
    active = refs[-1]

    @pl.when(pl.program_id(0) == 0)
    def _():
        picked, slots = chosen_ref.shape
        latents = active.shape[1]
        value = jnp.maximum(chosen_ref[...] + added_ref[...], 0.0)
        ids = lax.broadcasted_iota(jnp.int32, (latents, slots), 0)
        dense = jnp.zeros((latents, slots), F32)
        for p in range(picked):
            dense = jnp.where(ids == picks_ref[p:p + 1, :], value[p:p + 1, :], dense)
        active[...] = dense.T.astype(BF16)

    part = jnp.dot(active[...], dec_ref[...], preferred_element_type=F32).astype(BF16)
    first = 0
    for ref in refs[:-1]:
        ref[...] = part[first:first + ref.shape[0]]
        first += ref.shape[0]


def decode(chosen, added, picks, weight, sizes):
    picked, slots = chosen.shape
    latents, width = weight.shape
    return call(
        decode_kernel,
        "decode",
        (width // BLOCK,),
        [
            pl.BlockSpec((picked, slots), lambda j: (0, 0)),
            pl.BlockSpec((picked, slots), lambda j: (0, 0)),
            pl.BlockSpec((picked, slots), lambda j: (0, 0)),
            pl.BlockSpec((latents, BLOCK), lambda j: (0, j)),
        ],
        [pl.BlockSpec((size, BLOCK), lambda j: (0, j)) for size in sizes],
        [jax.ShapeDtypeStruct((size, width), BF16) for size in sizes],
        [pltpu.VMEM((slots, latents), BF16)],
    )(chosen, added, picks, weight)


def combine_kernel(spread_ref, *refs):
    parts = jnp.concatenate([ref[...] for ref in refs[:-1]], axis=0)
    total = jnp.dot(spread_ref[...], parts, preferred_element_type=F32)
    refs[-1][...] = total.astype(refs[-1].dtype)


def combine(spread, blocks, cap, first, width, dtype=BF16):
    rows, slots = spread.shape
    step = math.gcd(math.gcd(first, width), 1024)
    skip = first // step
    return call(
        combine_kernel,
        "combine",
        (width // step,),
        [pl.BlockSpec((rows, slots), lambda j: (0, 0))]
        + [pl.BlockSpec((cap, step), lambda j, at=at: (at, j + skip)) for _, at in blocks],
        pl.BlockSpec((rows, step), lambda j: (0, j)),
        jax.ShapeDtypeStruct((rows, width), dtype),
    )(spread, *(array for array, _ in blocks))


def spread_kernel(slots_ref, meta_ref, spread_ref):
    rows = spread_ref.shape[0]
    extra = meta_ref[...].astype(F32)
    hit = (extra[:, 0:1] == slots_ref[0:1, :]) | (extra[:, 1:2] == slots_ref[0:1, :])
    earlier = lax.broadcasted_iota(jnp.int32, (rows, rows), 1) < lax.broadcasted_iota(
        jnp.int32, (rows, rows), 0
    )
    rank = jnp.dot(
        jnp.where(earlier, 1.0, 0.0).astype(BF16),
        jnp.where(hit, 1.0, 0.0).astype(BF16),
        preferred_element_type=F32,
    )
    spread = jnp.where(hit & (rank == slots_ref[1:2, :]), 1.0, 0.0)
    spread_ref[...] = spread.astype(BF16)


def spread_of(slots, meta):
    return call(
        spread_kernel,
        "spread",
        (),
        [pl.BlockSpec(memory_space=pltpu.VMEM)] * 2,
        pl.BlockSpec(memory_space=pltpu.VMEM),
        jax.ShapeDtypeStruct((meta.shape[0], slots.shape[1]), BF16),
    )(slots, meta)


def line_on_device(tokens, dec_bias, routes, latent_picks, enc_weight, dec_weight, enc_bias):
    rows, width = tokens.shape
    top = routes.shape[1]
    picked = latent_picks.shape[2]
    blk_count = lax.axis_size("blocks")
    cap = max(2, 2 * rows * top // blk_count)
    me = lax.axis_index("blocks")
    plane, inner = me // INNER, me % INNER

    flat_picks = latent_picks.reshape(rows, top * picked)
    meta = jnp.concatenate([routes, flat_picks // 32, flat_picks % 32], axis=1).astype(BF16)
    meta = jnp.pad(meta, ((0, 0), (0, EXTRA - meta.shape[1])))
    own = jnp.concatenate([tokens, meta], axis=1)
    offset = jnp.pad(dec_bias, (0, EXTRA))[None, :]
    slot = jnp.arange(INNER * cap, dtype=jnp.int32)

    def slots_in(which):
        named = jnp.stack([which * INNER + ((slot // cap) ^ inner), slot % cap]).astype(F32)
        return jnp.pad(named, ((0, 6), (0, 0)))

    slots = slots_in(plane)
    bias = jnp.where(lax.axis_index("dp") == 0, enc_bias, 0.0)
    me_value = me.astype(F32).reshape(1, 1)
    enc, dec = enc_weight[0], dec_weight[0]

    with jax.named_scope("rows_ends"):
        by_one = move(own, ENDS)
    with jax.named_scope("rows_middle"):
        by_two = move(own, MIDDLE)
    groups = {0: (own,)}

    def exchange(pieces, name):
        moved = [pieces[0]]
        for j in range(1, INNER):
            with jax.named_scope(f"{name}_{j}"):
                moved.append(move(pieces[j], FLIPS[j]))
        return moved

    def all_after(values, *earlier):
        values = tuple(values)
        return lax.optimization_barrier((*values, *earlier))[:len(values)]

    def send_out(t):
        spread, pieces = dispatch(groups[t], offset, slots, cap)
        return spread, exchange(pieces, f"out_{t}")

    def encoded(t, pieces):
        chosen, picks = encode(pieces, enc, bias, me_value, cap, picked)
        with jax.named_scope(f"sums_{t}"):
            added = lax.ppermute(chosen, "dp", [(0, 1), (1, 0)])
        return picks, chosen, added

    def decoded(picks, chosen, added, sizes=(cap,) * INNER):
        return decode(chosen, added, picks, dec, sizes)

    def leave(t, pieces):
        return exchange(pieces, f"back_{t}")

    def combined(spread, pieces, shares):
        sums, first = [], 0
        for share in shares:
            size = width * share // sum(shares)
            sums.append(combine(spread, [(piece, 0) for piece in pieces], cap, first, size))
            first += size
        return sums

    def plus(a, b):
        return (a.astype(F32) + b.astype(F32)).astype(BF16)

    spreads, parts = {}, {}
    spreads[0], arrived = send_out(0)
    spread_next = spread_of(slots_in(plane ^ 1), meta)

    picks, chosen, added = encoded(0, arrived)
    added = after(added, chosen)
    by_one, by_two = all_after((by_one, by_two), added)
    with jax.named_scope("rows_outward_two"):
        to_ends_two = move(by_two, OUTWARD)
    with jax.named_scope("rows_middle_far"):
        by_three = move(by_one, MIDDLE)
    groups[1] = (by_one,)
    spreads[1], arrived = send_out(1)
    parts[0] = decoded(picks, chosen, after(added, spreads[1]))

    picks, chosen, added = encoded(1, all_after(arrived, *parts[0]))
    (parts1,) = decoded(picks, chosen, added, (INNER * cap,))
    with jax.named_scope("parts_inward"):
        inward = move(parts1, INWARD)
    to_ends_two = after(to_ends_two, parts1)
    by_three = after(by_three, to_ends_two)
    with jax.named_scope("rows_outward_far"):
        to_ends_three = move(by_three, OUTWARD)
    groups[2] = (by_two, to_ends_two)
    spreads[2], arrived = send_out(2)

    picks, chosen, added = encoded(2, arrived)
    parts[2] = decoded(picks, chosen, added)
    returned2 = leave(2, parts[2])
    to_ends_three = after(to_ends_three, *parts[2])
    returned2[1] = after(returned2[1], to_ends_three)
    with jax.named_scope("parts_outward"):
        outward = move(after(parts1, to_ends_three), OUTWARD)
    groups[3] = (by_three, after(to_ends_three, returned2[1]))
    spreads[3], arrived = send_out(3)
    arrived[1] = after(arrived[1], spreads[3])
    arrived[2] = after(arrived[2], arrived[1])
    inward = after(inward, arrived[2])
    arrived[3] = after(arrived[3], inward)

    picks, chosen, added = encoded(3, arrived)
    parts[3] = decoded(picks, chosen, added)
    returned3 = leave(3, parts[3])
    back2 = combined(spreads[2], all_after(returned2, *parts[3]), TWO_SHARES)
    from_two = []
    for i, value in enumerate(back2):
        with jax.named_scope(f"sum_inward_two_{i}"):
            from_two.append(move(value, INWARD))
    twos, ones = [], []

    def two_on(i, *earlier):
        from_two[i] = after(from_two[i], *earlier)
        with jax.named_scope(f"sum_middle_two_{i}"):
            twos.append(move(plus(back2[i], from_two[i]), MIDDLE))

    returned3[2] = after(returned3[2], *back2)
    outward = after(outward, returned3[2])
    two_on(0, outward)
    returned3 = all_after(returned3, from_two[0])
    back3 = combined(spreads[3], returned3, FAR_SHARES)
    two_on(1, *back3)
    twos[0] = after(twos[0], from_two[1])
    from_far = []
    for i, value in enumerate(back3):
        with jax.named_scope(f"sum_inward_far_{i}"):
            from_far.append(move(value, INWARD))

    near = inward + outward
    pieces = []
    for j in range(1, INNER):
        pieces.append(jnp.concatenate([parts[0][j], near[j * cap:(j + 1) * cap]], axis=0))
    pieces = exchange([None, *all_after(pieces, *returned3)], "back_near")

    def skip_on(i, *earlier):
        from_far[i] = after(from_far[i], *earlier)
        with jax.named_scope(f"sum_skip_far_{i}"):
            ones.append(move(plus(back3[i], from_far[i]), SKIP))

    skip_on(0, pieces[2], twos[0])
    twos[1] = after(twos[1], from_far[0])
    pieces[3] = after(pieces[3], twos[1])
    skip_on(1, pieces[3], ones[0])
    pieces[1] = after(pieces[1], from_far[1])
    blocks = [(parts[0][0], 0)] + [(piece, 0) for piece in pieces[1:]]
    blocks += [(near, 0)] + [(piece, 1) for piece in pieces[1:]]
    near = combine(
        jnp.concatenate([spreads[0], spread_next], axis=1), blocks, cap, 0, width, F32
    )
    ones = all_after(ones, near)
    near = near + dec_bias + jnp.concatenate(twos, axis=1).astype(F32)
    return (near + jnp.concatenate(ones, axis=1).astype(F32)).astype(BF16)


def solution(mesh):
    in_specs = (
        P("blocks", "dp"),
        P("dp"),
        P("blocks", None),
        P("blocks", None, None),
        P("blocks", "dp", None),
        P("blocks", None, "dp"),
        P("blocks", None),
    )
    on_device = line_on_device if mesh.shape["blocks"] == OUTER * INNER else flat_on_device
    return jax.shard_map(
        on_device, mesh=mesh, in_specs=in_specs, out_specs=P("blocks", "dp"), check_vma=False
    )
```

```python
import functools
import math

import jax
import jax.numpy as jnp
from jax import lax
from jax.experimental import pallas as pl
from jax.experimental.pallas import tpu as pltpu
from jax.sharding import PartitionSpec as P

BACK_CHUNKS = (1, 1, 1, 1)
TWO_SHARES = (1, 1)
FAR_SHARES = (3, 5)
INNER = 4
OUTER = 4
EXTRA = 128
BLOCK = 2048
VMEM = 24 * 1024 * 1024
F32 = jnp.float32
BF16 = jnp.bfloat16


def flat_on_device(tokens, dec_bias, routes, latent_picks, enc_weight, dec_weight, enc_bias):
    tok_rows, quarter = tokens.shape
    top_blocks = routes.shape[1]
    pick_count = latent_picks.shape[2]
    latents = enc_weight.shape[2]
    blk_count = lax.axis_size("blocks")
    capacity = max(2, 2 * tok_rows * top_blocks // blk_count)
    slot_count = blk_count * capacity
    pair_count = tok_rows * top_blocks
    centered = (tokens.astype(F32) - dec_bias).astype(BF16)
    owners = routes.reshape(pair_count)
    onehot = (owners[:, None] == jnp.arange(blk_count, dtype=jnp.int32)[None, :]).astype(jnp.int32)
    slot_rank = jnp.sum(jnp.cumsum(onehot, axis=0) * onehot, axis=1) - 1
    target = owners * capacity + slot_rank
    placing = jnp.arange(slot_count, dtype=jnp.int32)[:, None] == target[None, :]
    place_half = placing.astype(BF16)
    paired = jnp.repeat(centered, top_blocks, axis=0)
    outgoing = jnp.dot(place_half, paired, preferred_element_type=F32).astype(BF16)
    outgoing = outgoing.reshape(blk_count, capacity, quarter)
    sent_picks = jnp.dot(
        placing.astype(F32),
        latent_picks.reshape(pair_count, pick_count).astype(F32),
        precision=lax.Precision.HIGHEST,
    ).astype(jnp.int32)
    sent_picks = sent_picks.reshape(blk_count, capacity, pick_count)
    lat_ids = jnp.arange(latents, dtype=jnp.int32)
    arrived = lax.all_to_all(outgoing, "blocks", split_axis=0, concat_axis=0, tiled=True)
    chosen = lax.all_to_all(sent_picks, "blocks", split_axis=0, concat_axis=0, tiled=True)
    flat_rows = arrived.reshape(slot_count, quarter)
    chosen_ids = chosen.reshape(slot_count, pick_count)
    partial_value = jnp.dot(flat_rows, enc_weight[0], preferred_element_type=F32)
    summed = lax.psum(partial_value, "dp") + enc_bias[0][None, :]
    keep_mask = jnp.any(chosen_ids[:, :, None] == lat_ids[None, None, :], axis=1)
    active = jnp.where(keep_mask, jnp.maximum(summed, 0.0), 0.0).astype(BF16)
    partial_out = jnp.dot(active, dec_weight[0], preferred_element_type=F32).astype(BF16)
    partial_out = partial_out.reshape(blk_count, capacity, quarter)
    returned = lax.all_to_all(partial_out, "blocks", split_axis=0, concat_axis=0, tiled=True)
    back_rows = returned.reshape(slot_count, quarter)
    per_pair = jnp.einsum("sp,sd->pd", place_half, back_rows, preferred_element_type=F32)
    summed_out = per_pair.reshape(tok_rows, top_blocks, quarter).sum(axis=1) + dec_bias
    return summed_out.astype(BF16)


def outer_pairs(pairs):
    return [(a * INNER + i, b * INNER + i) for a, b in pairs for i in range(INNER)]


def inner_pairs(flip):
    return [(i, i ^ flip) for i in range(OUTER * INNER)]


ENDS = outer_pairs([(0, 1), (1, 0), (2, 3), (3, 2)])
MIDDLE = outer_pairs([(1, 2), (2, 1)])
OUTWARD = outer_pairs([(1, 0), (2, 3)])
INWARD = outer_pairs([(0, 1), (3, 2)])
SKIP = outer_pairs([(1, 3), (2, 0)])
FLIPS = {1: inner_pairs(1), 2: inner_pairs(2), 3: inner_pairs(3)}


def move(value, pairs):
    return lax.ppermute(value, "blocks", pairs)


def after(value, *others):
    return lax.optimization_barrier((value, *others))[0]


def call(kernel, name, grid, in_specs, out_specs, out_shape, scratch=()):
    return pl.pallas_call(
        kernel,
        name=name,
        grid=grid,
        in_specs=in_specs,
        out_specs=out_specs,
        out_shape=out_shape,
        scratch_shapes=scratch,
        compiler_params=pltpu.CompilerParams(vmem_limit_bytes=VMEM),
        cost_estimate=pl.CostEstimate(flops=0, bytes_accessed=0, transcendentals=0),
    )


def dispatch_kernel(cap, n, slots_ref, offset_ref, *refs):
    value_refs, (spread_ref, *out_refs) = refs[:n], refs[n:]
    rows, wide = value_refs[0].shape
    extra = value_refs[0][:, wide - EXTRA:].astype(F32)
    for ref in value_refs[1:]:
        extra = extra + ref[:, wide - EXTRA:].astype(F32)
    hit = (extra[:, 0:1] == slots_ref[0:1, :]) | (extra[:, 1:2] == slots_ref[0:1, :])
    earlier = lax.broadcasted_iota(jnp.int32, (rows, rows), 1) < lax.broadcasted_iota(
        jnp.int32, (rows, rows), 0
    )
    rank = jnp.dot(
        jnp.where(earlier, 1.0, 0.0).astype(BF16),
        jnp.where(hit, 1.0, 0.0).astype(BF16),
        preferred_element_type=F32,
    )
    spread = jnp.where(hit & (rank == slots_ref[1:2, :]), 1.0, 0.0)
    spread_ref[...] = spread.astype(BF16)
    value = value_refs[0][...]
    for ref in value_refs[1:]:
        value = value + ref[...]
    place = spread.T.astype(BF16)
    moved = (jnp.dot(place, value, preferred_element_type=F32) - offset_ref[...]).astype(BF16)
    for j, ref in enumerate(out_refs):
        ref[...] = moved[j * cap:(j + 1) * cap]


def dispatch(values, offset, slots, cap):
    rows, wide = values[0].shape
    spread, *pieces = call(
        functools.partial(dispatch_kernel, cap, len(values)),
        "dispatch",
        (),
        [pl.BlockSpec(memory_space=pltpu.VMEM)] * (2 + len(values)),
        [pl.BlockSpec(memory_space=pltpu.VMEM)] * (1 + INNER),
        [jax.ShapeDtypeStruct((rows, INNER * cap), BF16)]
        + [jax.ShapeDtypeStruct((cap, wide), BF16)] * INNER,
    )(slots, offset, *values)
    return spread, pieces


def encode_kernel(picked, piece_refs, extra_refs, enc_ref, bias_ref, me_ref, chosen_ref, picks_ref, total):
    k = pl.program_id(0)

    @pl.when(k == 0)
    def _():
        total[...] = jnp.broadcast_to(bias_ref[...], total.shape)

    mine = jnp.concatenate([ref[...] for ref in piece_refs], axis=0)
    total[...] += jnp.dot(mine, enc_ref[...], preferred_element_type=F32)

    @pl.when(k == pl.num_programs(0) - 1)
    def _():
        extra = jnp.concatenate([ref[...] for ref in extra_refs], axis=0).astype(F32)
        size = 2 * picked
        both = extra[:, 2:2 + size] * 32.0 + extra[:, 2 + size:2 + 2 * size]
        both = both.astype(jnp.int32)
        picks = jnp.where(extra[:, 0:1] == me_ref[0, 0], both[:, :picked], both[:, picked:])
        slots, latents = total.shape
        picks = jnp.concatenate([picks, jnp.zeros((slots, EXTRA - picked), jnp.int32)], axis=1)
        group, lane = picks // EXTRA, picks % EXTRA
        values = jnp.zeros((slots, EXTRA), F32)
        for g in range(latents // EXTRA):
            here = total[:, g * EXTRA:(g + 1) * EXTRA]
            values = jnp.where(group == g, jnp.take_along_axis(here, lane, axis=1), values)
        chosen_ref[...] = values.T[:picked]
        picks_ref[...] = picks.astype(F32).T[:picked].astype(jnp.int32)


def encode(pieces, weight, bias, me, cap, picked):
    width, latents = weight.shape
    slots = INNER * cap
    last = width // EXTRA

    def kernel(*refs):
        encode_kernel(picked, refs[:INNER], refs[INNER:2 * INNER], *refs[2 * INNER:])

    return call(
        kernel,
        "encode",
        (width // BLOCK,),
        [pl.BlockSpec((cap, BLOCK), lambda k: (0, k))] * INNER
        + [pl.BlockSpec((cap, EXTRA), lambda k: (0, last))] * INNER
        + [
            pl.BlockSpec((BLOCK, latents), lambda k: (k, 0)),
            pl.BlockSpec((1, latents), lambda k: (0, 0)),
            pl.BlockSpec(memory_space=pltpu.SMEM),
        ],
        [
            pl.BlockSpec((picked, slots), lambda k: (0, 0)),
            pl.BlockSpec((picked, slots), lambda k: (0, 0)),
        ],
        [
            jax.ShapeDtypeStruct((picked, slots), F32),
            jax.ShapeDtypeStruct((picked, slots), jnp.int32),
        ],
        [pltpu.VMEM((slots, latents), F32)],
    )(*pieces, *pieces, weight, bias, me)


def decode_kernel(chosen_ref, added_ref, picks_ref, dec_ref, *refs):
    active = refs[-1]

    @pl.when(pl.program_id(0) == 0)
    def _():
        picked, slots = chosen_ref.shape
        latents = active.shape[1]
        value = jnp.maximum(chosen_ref[...] + added_ref[...], 0.0)
        ids = lax.broadcasted_iota(jnp.int32, (latents, slots), 0)
        dense = jnp.zeros((latents, slots), F32)
        for p in range(picked):
            dense = jnp.where(ids == picks_ref[p:p + 1, :], value[p:p + 1, :], dense)
        active[...] = dense.T.astype(BF16)

    part = jnp.dot(active[...], dec_ref[...], preferred_element_type=F32).astype(BF16)
    first = 0
    for ref in refs[:-1]:
        ref[...] = part[first:first + ref.shape[0]]
        first += ref.shape[0]


def decode(chosen, added, picks, weight, sizes):
    picked, slots = chosen.shape
    latents, width = weight.shape
    return call(
        decode_kernel,
        "decode",
        (width // BLOCK,),
        [
            pl.BlockSpec((picked, slots), lambda j: (0, 0)),
            pl.BlockSpec((picked, slots), lambda j: (0, 0)),
            pl.BlockSpec((picked, slots), lambda j: (0, 0)),
            pl.BlockSpec((latents, BLOCK), lambda j: (0, j)),
        ],
        [pl.BlockSpec((size, BLOCK), lambda j: (0, j)) for size in sizes],
        [jax.ShapeDtypeStruct((size, width), BF16) for size in sizes],
        [pltpu.VMEM((slots, latents), BF16)],
    )(chosen, added, picks, weight)


def combine_kernel(spread_ref, *refs):
    parts = jnp.concatenate([ref[...] for ref in refs[:-1]], axis=0)
    total = jnp.dot(spread_ref[...], parts, preferred_element_type=F32)
    refs[-1][...] = total.astype(refs[-1].dtype)


def combine(spread, blocks, cap, first, width, dtype=BF16):
    rows, slots = spread.shape
    step = math.gcd(math.gcd(first, width), 1024)
    skip = first // step
    return call(
        combine_kernel,
        "combine",
        (width // step,),
        [pl.BlockSpec((rows, slots), lambda j: (0, 0))]
        + [pl.BlockSpec((cap, step), lambda j, at=at: (at, j + skip)) for _, at in blocks],
        pl.BlockSpec((rows, step), lambda j: (0, j)),
        jax.ShapeDtypeStruct((rows, width), dtype),
    )(spread, *(array for array, _ in blocks))


def spread_kernel(slots_ref, meta_ref, spread_ref):
    rows = spread_ref.shape[0]
    extra = meta_ref[...].astype(F32)
    hit = (extra[:, 0:1] == slots_ref[0:1, :]) | (extra[:, 1:2] == slots_ref[0:1, :])
    earlier = lax.broadcasted_iota(jnp.int32, (rows, rows), 1) < lax.broadcasted_iota(
        jnp.int32, (rows, rows), 0
    )
    rank = jnp.dot(
        jnp.where(earlier, 1.0, 0.0).astype(BF16),
        jnp.where(hit, 1.0, 0.0).astype(BF16),
        preferred_element_type=F32,
    )
    spread = jnp.where(hit & (rank == slots_ref[1:2, :]), 1.0, 0.0)
    spread_ref[...] = spread.astype(BF16)


def spread_of(slots, meta):
    return call(
        spread_kernel,
        "spread",
        (),
        [pl.BlockSpec(memory_space=pltpu.VMEM)] * 2,
        pl.BlockSpec(memory_space=pltpu.VMEM),
        jax.ShapeDtypeStruct((meta.shape[0], slots.shape[1]), BF16),
    )(slots, meta)


def line_on_device(tokens, dec_bias, routes, latent_picks, enc_weight, dec_weight, enc_bias):
    rows, width = tokens.shape
    top = routes.shape[1]
    picked = latent_picks.shape[2]
    blk_count = lax.axis_size("blocks")
    cap = max(2, 2 * rows * top // blk_count)
    me = lax.axis_index("blocks")
    plane, inner = me // INNER, me % INNER

    flat_picks = latent_picks.reshape(rows, top * picked)
    meta = jnp.concatenate([routes, flat_picks // 32, flat_picks % 32], axis=1).astype(BF16)
    meta = jnp.pad(meta, ((0, 0), (0, EXTRA - meta.shape[1])))
    own = jnp.concatenate([tokens, meta], axis=1)
    offset = jnp.pad(dec_bias, (0, EXTRA))[None, :]
    slot = jnp.arange(INNER * cap, dtype=jnp.int32)

    def slots_in(which):
        named = jnp.stack([which * INNER + ((slot // cap) ^ inner), slot % cap]).astype(F32)
        return jnp.pad(named, ((0, 6), (0, 0)))

    slots = slots_in(plane)
    bias = jnp.where(lax.axis_index("dp") == 0, enc_bias, 0.0)
    me_value = me.astype(F32).reshape(1, 1)
    enc, dec = enc_weight[0], dec_weight[0]

    with jax.named_scope("rows_ends"):
        by_one = move(own, ENDS)
    with jax.named_scope("rows_middle"):
        by_two = move(own, MIDDLE)
    groups = {0: (own,)}

    def exchange(pieces, name):
        moved = [pieces[0]]
        for j in range(1, INNER):
            with jax.named_scope(f"{name}_{j}"):
                moved.append(move(pieces[j], FLIPS[j]))
        return moved

    def all_after(values, *earlier):
        values = tuple(values)
        return lax.optimization_barrier((*values, *earlier))[:len(values)]

    def send_out(t):
        spread, pieces = dispatch(groups[t], offset, slots, cap)
        return spread, exchange(pieces, f"out_{t}")

    def encoded(t, pieces):
        chosen, picks = encode(pieces, enc, bias, me_value, cap, picked)
        with jax.named_scope(f"sums_{t}"):
            added = lax.ppermute(chosen, "dp", [(0, 1), (1, 0)])
        return picks, chosen, added

    def decoded(picks, chosen, added, sizes=(cap,) * INNER):
        return decode(chosen, added, picks, dec, sizes)

    def leave(t, pieces):
        return exchange(pieces, f"back_{t}")

    def combined(spread, pieces, shares):
        sums, first = [], 0
        for share in shares:
            size = width * share // sum(shares)
            sums.append(combine(spread, [(piece, 0) for piece in pieces], cap, first, size))
            first += size
        return sums

    def plus(a, b):
        return (a.astype(F32) + b.astype(F32)).astype(BF16)

    spreads, parts = {}, {}
    spreads[0], arrived = send_out(0)
    spread_next = spread_of(slots_in(plane ^ 1), meta)

    picks, chosen, added = encoded(0, arrived)
    added = after(added, chosen)
    by_one, by_two = all_after((by_one, by_two), added)
    with jax.named_scope("rows_outward_two"):
        to_ends_two = move(by_two, OUTWARD)
    with jax.named_scope("rows_middle_far"):
        by_three = move(by_one, MIDDLE)
    groups[1] = (by_one,)
    spreads[1], arrived = send_out(1)
    parts[0] = decoded(picks, chosen, after(added, spreads[1]))

    picks, chosen, added = encoded(1, all_after(arrived, *parts[0]))
    (parts1,) = decoded(picks, chosen, added, (INNER * cap,))
    with jax.named_scope("parts_inward"):
        inward = move(parts1, INWARD)
    to_ends_two = after(to_ends_two, parts1)
    by_three = after(by_three, to_ends_two)
    with jax.named_scope("rows_outward_far"):
        to_ends_three = move(by_three, OUTWARD)
    groups[2] = (by_two, to_ends_two)
    spreads[2], arrived = send_out(2)

    picks, chosen, added = encoded(2, arrived)
    parts[2] = decoded(picks, chosen, added)
    returned2 = leave(2, parts[2])
    to_ends_three = after(to_ends_three, *parts[2])
    returned2[1] = after(returned2[1], to_ends_three)
    with jax.named_scope("parts_outward"):
        outward = move(after(parts1, to_ends_three), OUTWARD)
    groups[3] = (by_three, after(to_ends_three, returned2[1]))
    spreads[3], arrived = send_out(3)
    arrived[1] = after(arrived[1], spreads[3])
    arrived[2] = after(arrived[2], arrived[1])
    inward = after(inward, arrived[2])
    arrived[3] = after(arrived[3], inward)

    picks, chosen, added = encoded(3, arrived)
    parts[3] = decoded(picks, chosen, added)
    returned3 = leave(3, parts[3])
    back2 = combined(spreads[2], all_after(returned2, *parts[3]), TWO_SHARES)
    from_two = []
    for i, value in enumerate(back2):
        with jax.named_scope(f"sum_inward_two_{i}"):
            from_two.append(move(value, INWARD))
    twos, ones = [], []

    def two_on(i, *earlier):
        from_two[i] = after(from_two[i], *earlier)
        with jax.named_scope(f"sum_middle_two_{i}"):
            twos.append(move(plus(back2[i], from_two[i]), MIDDLE))

    returned3[2] = after(returned3[2], *back2)
    outward = after(outward, returned3[2])
    two_on(0, outward)
    returned3 = all_after(returned3, from_two[0])
    back3 = combined(spreads[3], returned3, FAR_SHARES)
    two_on(1, *back3)
    twos[0] = after(twos[0], from_two[1])
    from_far = []
    for i, value in enumerate(back3):
        with jax.named_scope(f"sum_inward_far_{i}"):
            from_far.append(move(value, INWARD))

    near = inward + outward
    pieces = []
    for j in range(1, INNER):
        pieces.append(jnp.concatenate([parts[0][j], near[j * cap:(j + 1) * cap]], axis=0))
    pieces = exchange([None, *all_after(pieces, *returned3)], "back_near")

    def skip_on(i, *earlier):
        from_far[i] = after(from_far[i], *earlier)
        with jax.named_scope(f"sum_skip_far_{i}"):
            ones.append(move(plus(back3[i], from_far[i]), SKIP))

    skip_on(0, pieces[2], twos[0])
    twos[1] = after(twos[1], from_far[0])
    pieces[3] = after(pieces[3], twos[1])
    skip_on(1, pieces[3], ones[0])
    pieces[1] = after(pieces[1], from_far[1])
    blocks = [(parts[0][0], 0)] + [(piece, 0) for piece in pieces[1:]]
    blocks += [(near, 0)] + [(piece, 1) for piece in pieces[1:]]
    near = combine(
        jnp.concatenate([spreads[0], spread_next], axis=1), blocks, cap, 0, width, F32
    )
    ones = all_after(ones, near)
    near = near + dec_bias + jnp.concatenate(twos, axis=1).astype(F32)
    return (near + jnp.concatenate(ones, axis=1).astype(F32)).astype(BF16)


def solution(mesh):
    in_specs = (
        P("blocks", "dp"),
        P("dp"),
        P("blocks", None),
        P("blocks", None, None),
        P("blocks", "dp", None),
        P("blocks", None, "dp"),
        P("blocks", None),
    )
    on_device = line_on_device if mesh.shape["blocks"] == OUTER * INNER else flat_on_device
    return jax.shard_map(
        on_device, mesh=mesh, in_specs=in_specs, out_specs=P("blocks", "dp"), check_vma=False
    )
```
